256 devices in a mesh: alpha: 16 (over z_hi, x), beta: 4 (over z_lo, core), chol: 4 (over y).
Axes of the slice: x: 4, y: 4, z: 8 (z_hi: 4, z_lo: 2; z = z_hi * 2 + z_lo), core: 2. Of those that a mesh axis runs over, the one named last changes fastest.
Arguments:
- ci_vector: bfloat16 [2048, 4096], P('alpha', 'beta'), may hold values from -6 to 6
- a_tiles: bfloat16 [64, 16, 6, 128, 128], P('chol', 'alpha'), may hold values from -0.21875 to 0.21875
- a_source: int32 [16, 6], P('alpha'), may hold values from 0 to 15
- a_sign: int32 [16, 6], P('alpha'), may hold values from -1 to 1, as said below
- b_tiles: bfloat16 [64, 32, 3, 128, 128], P('chol', 'beta'), may hold values from -0.0390625 to 0.0390625
- b_source: int32 [32, 3], P('beta'), may hold values from 0 to 31
- b_sign: int32 [32, 3], P('beta'), may hold values from -1 to 1, as said below
Outputs:
- sigma_out: bfloat16 [2048, 4096], P('alpha', ('beta', 'chol'))
The draws below stay inside these ranges and needn't reach their ends.
Inputs may be any that keep to these rules, and one draw needn't show every extreme that they name: `a_sign`: in each row the first c slots are live with sign +1 or -1 and the rest are 0, c between 1 and 6; some row has all 6 slots live. `b_sign`: in each row the first c slots are live with sign +1 or -1 and the rest are 0, c between 1 and 3; some row has all 3 slots live.
All inputs are finite; a program needn't handle non-finite values.
Results may differ from the reference program's by a relative error of at most 0.0049.
Values may be sent and summed in bfloat16 or wider, within the bound.
No kernel may reach another device: no remote copies, remote signals or barrier semaphores. Data moves between devices by JAX's collectives and lax.ppermute only.
A program may use at most 128 MiB of HBM per device.

```python
import jax
import jax.numpy as jnp
from jax import lax

STR_BLK = 128
KA = 6
KB = 3
NQ = 64
NAB = 16
NBB = 32
NA = 2048
NB = 4096


def live_signs(key, row_count, slot_count):
    key_count, key_full, key_flip = jax.random.split(key, 3)
    live_count = jax.random.randint(key_count, (row_count,), 1, slot_count + 1)
    full_row = jax.random.randint(key_full, (), 0, row_count)
    live_count = jnp.where(jnp.arange(row_count) == full_row, slot_count, live_count)
    sign_flips = jax.random.randint(key_flip, (row_count, slot_count), 0, 2) * 2 - 1
    return jnp.where(jnp.arange(slot_count)[None, :] < live_count[:, None], sign_flips, 0).astype(jnp.int32)


def draw_a_sign(key, part):
    key = jax.random.fold_in(key, 11)
    return live_signs(key, NAB, KA)


def draw_b_sign(key, part):
    key = jax.random.fold_in(key, 23)
    return live_signs(key, NBB, KB)


def place_ends(result, rng, low, top_value):
    dims = result.shape
    index_at = [jax.random.randint(jax.random.fold_in(rng, axis), (), 0, dims[axis]) for axis in range(len(dims))]
    result = result.at[tuple(index_at)].set(low)
    longest = dims.index(max(dims))
    index_at[longest] = (index_at[longest] + 1) % dims[longest]
    return result.at[tuple(index_at)].set(top_value)


def steps_of(own_key, dims, pieces, low, high):
    gain = 1.0
    for dim, shards_of in pieces:
        steps = jax.random.uniform(jax.random.fold_in(jax.random.fold_in(own_key, 6), dim), (shards_of,), jnp.float32, low / len(pieces), high / len(pieces))
        gain = gain * jnp.repeat(jnp.exp(steps), dims[dim] // shards_of).reshape((-1,) + (1,) * (len(dims) - 1 - dim))
    return gain


def scatter_about(key, shape, deviation, most, cuts=(), kind=jnp.bfloat16):
    factor_of = steps_of(key, shape, cuts, -0.22, 0.18) if cuts else 1.0
    result = jax.random.normal(key, shape, jnp.float32) * deviation * factor_of
    return jnp.minimum(jnp.maximum(result, -most), most).astype(kind)


def setup_inputs(seed: int = 0) -> dict:
    seeds = jax.random.split(jax.random.key(seed), 8)
    ci_vector = scatter_about(seeds[0], (NA, NB), 1.0, 6.0, ((0, 16), (1, 4)))
    a_tiles = scatter_about(seeds[1], (NQ, NAB, KA, STR_BLK, STR_BLK), (STR_BLK * KA) ** -0.5, 0.21875, ((0, 4), (1, 16)))
    a_source = place_ends(jax.random.randint(seeds[2], (NAB, KA), 0, NAB), jax.random.fold_in(seeds[2], 1), 0, NAB - 1).astype(jnp.int32)
    a_sign = draw_a_sign(jax.random.fold_in(seeds[7], 71), 0)
    b_tiles = scatter_about(seeds[4], (NQ, NBB, KB, STR_BLK, STR_BLK), (STR_BLK * KB * NQ) ** -0.5, 0.0390625, ((0, 4), (1, 4)))
    b_source = place_ends(jax.random.randint(seeds[5], (NBB, KB), 0, NBB), jax.random.fold_in(seeds[5], 1), 0, NBB - 1).astype(jnp.int32)
    b_sign = draw_b_sign(jax.random.fold_in(seeds[7], 71), 0)
    return {"ci_vector": ci_vector, "a_tiles": a_tiles, "a_source": a_source, "a_sign": a_sign, "b_tiles": b_tiles, "b_source": b_source, "b_sign": b_sign}


def reference(ci_vector, a_tiles, a_source, a_sign, b_tiles, b_source, b_sign):
    row_blocks = ci_vector.reshape(NAB, STR_BLK, NB)
    picked = row_blocks[a_source.astype(jnp.int32)].astype(jnp.float32)
    alpha_signs = a_sign.astype(jnp.float32)
    beta_signs = b_sign.astype(jnp.float32)

    def add_vector(running, pair):
        alpha_tile, beta_tile = pair
        weighted = alpha_tile.astype(jnp.float32) * alpha_signs[:, :, None, None]
        panel = jnp.einsum("tkij,tkjn->tin", weighted, picked).astype(jnp.bfloat16)
        column_blocks = panel.reshape(NAB, STR_BLK, NBB, STR_BLK)
        chosen = column_blocks[:, :, b_source.astype(jnp.int32)].astype(jnp.float32)
        weighted_b = beta_tile.astype(jnp.float32) * beta_signs[:, :, None, None]
        return running + jnp.einsum("tiulm,ulrm->tiur", chosen, weighted_b), None

    start = jnp.zeros((NAB, STR_BLK, NBB, STR_BLK), jnp.float32)
    running, _ = lax.scan(add_vector, start, (a_tiles, b_tiles))
    return running.reshape(NA, NB).astype(jnp.bfloat16)
```

```python
import jax
import jax.numpy as jnp
from jax import lax
from jax.experimental import pallas as pl
from jax.experimental.pallas import tpu as pltpu
from jax.sharding import PartitionSpec as P

BLK = 128
VECTORS_PER_DOT = 2
VECTORS_PER_GROUP = 4
X_SIZE = 4
SMEM = pl.BlockSpec(memory_space=pltpu.SMEM)
VMEM = pl.BlockSpec(memory_space=pltpu.VMEM)
HBM = pl.BlockSpec(memory_space=pltpu.HBM)


def shifted(value, axis, size, moves_to):
    return lax.ppermute(value, axis, [(i, moves_to(i)) for i in range(size)])


def pick_kernel(place_ref, source_ref, sign_ref, own_ref, next_ref, prev_ref, far_low_ref, far_high_ref, out_ref):
    slots = source_ref.shape[1]
    alpha = place_ref[0]
    for k in range(slots):
        source = source_ref[0, k]
        sign = sign_ref[0, k].astype(jnp.float32).astype(out_ref.dtype)
        dz = lax.rem(source // X_SIZE - alpha // X_SIZE + 4, 4)
        dx = lax.rem(source % X_SIZE - alpha % X_SIZE + X_SIZE, X_SIZE)

        def put(ref, at, k=k, sign=sign):
            for half in range(2):
                out_ref[half, k * BLK : (k + 1) * BLK, :] = (
                    ref[at, :, half * BLK : (half + 1) * BLK] * sign
                )

        for distance, ref in ((0, own_ref), (1, next_ref), (3, prev_ref)):

            @pl.when(dx == distance)
            def _(ref=ref):
                put(ref, dz)

        @pl.when(jnp.logical_and(dx == 2, dz < 2))
        def _():
            put(far_low_ref, jnp.minimum(dz, 1))

        @pl.when(jnp.logical_and(dx == 2, dz >= 2))
        def _():
            put(far_high_ref, jnp.maximum(dz - 2, 0))


def choose(index, low, high, act):
    if high - low == 1:
        act(low)
        return
    middle = (low + high) // 2

    @pl.when(index < middle)
    def _():
        choose(index, low, middle, act)

    @pl.when(index >= middle)
    def _():
        choose(index, middle, high, act)


def contract_kernel(place_ref, source_ref, sign_ref, a_hbm, b_ref, *rest):
    units = rest[:16]
    own_ref, *piece_refs = rest[16:20]
    acc, tasks, a_ref, c_buf, b_buf, a_sem, c_sem, b_sem = rest[20:]
    pairs = sign_ref.shape[0] * sign_ref.shape[1]
    slots = sign_ref.shape[1]
    vectors, a_slots = a_ref.shape[:2]
    beta, chol = place_ref[1], place_ref[2]
    a_copy = pltpu.make_async_copy(a_hbm, a_ref, a_sem)
    a_copy.start()
    acc[...] = jnp.zeros_like(acc)

    count = jnp.int32(0)
    for pair in range(pairs):
        tasks[count] = pair
        count = count + jnp.where(sign_ref[pair // slots, pair % slots] != 0, 1, 0)
    steps = (count + 1) // 2

    def task_of(step, half):
        at = jnp.minimum(2 * step + half, count - 1)
        pair = tasks[at]
        u = pair // slots
        l = pair - u * slots
        return u, l

    def c_copy(unit, m, slot, half):
        return pltpu.make_async_copy(
            unit.at[m & 1], c_buf.at[slot, :, pl.ds(half * BLK, BLK)], c_sem.at[slot, half]
        )

    def b_copy(u, l, slot, half):
        return pltpu.make_async_copy(b_ref.at[:, u, l], b_buf.at[slot, half], b_sem.at[slot, half])

    def start(step, slot):
        for half in range(2):
            u, l = task_of(step, half)
            b_copy(u, l, slot, half).start()
            m = source_ref[u, l]
            distance = ((m >> 3) ^ beta) * 4 + (((m >> 1) - chol) & 3)
            choose(distance, 0, len(units), lambda i: c_copy(units[i], m, slot, half).start())

    @pl.when(steps > 0)
    def _():
        start(0, 0)

    a_copy.wait()

    def body(step, carry):
        slot = step & 1

        @pl.when(step + 1 < steps)
        def _():
            start(step + 1, 1 - slot)

        for half in range(2):
            c_copy(units[0], 0, slot, half).wait()
            b_copy(0, 0, slot, half).wait()
        sums = [jnp.zeros((BLK, BLK), jnp.float32) for _ in range(2)]
        for group in range(0, vectors, VECTORS_PER_GROUP):
            panels = []
            for first in range(group, group + VECTORS_PER_GROUP, VECTORS_PER_DOT):
                rows = [
                    jnp.concatenate([a_ref[q, k] for k in range(a_slots)], axis=1)
                    for q in range(first, first + VECTORS_PER_DOT)
                ]
                panel = jnp.dot(
                    jnp.concatenate(rows, axis=0), c_buf[slot], preferred_element_type=jnp.float32
                ).astype(jnp.bfloat16)
                panels += [panel[r * BLK : (r + 1) * BLK] for r in range(VECTORS_PER_DOT)]
            for half in range(2):
                left = [panel[:, half * BLK : (half + 1) * BLK] for panel in panels]
                right = [b_buf[slot, half, group + r] for r in range(VECTORS_PER_GROUP)]
                sums[half] += lax.dot_general(
                    jnp.concatenate(left, axis=1),
                    jnp.concatenate(right, axis=1),
                    (((1,), (1,)), ((), ())),
                    preferred_element_type=jnp.float32,
                )
        for half in range(2):
            u, l = task_of(step, half)
            live = 2 * step + half < count
            factor = jnp.where(live, sign_ref[u, l], 0).astype(jnp.float32)
            lanes = pl.ds(pl.multiple_of((u & 1) * BLK, BLK), BLK)
            acc[u >> 1, :, lanes] += factor * sums[half]
        return carry

    lax.fori_loop(0, steps, body, 0)
    own_ref[...] = acc[chol]
    for shift, piece_ref in enumerate(piece_refs, 1):
        piece_ref[...] = acc[(chol + shift) & 3].astype(piece_ref.dtype)


def contract(place, b_source, b_sign, a_tiles, b_tiles, units):
    vectors, blocks, slots = b_tiles.shape[:3]
    flops = 2 * a_tiles.size * blocks * slots * BLK + 2 * b_tiles.size * BLK
    moved = 2 * (b_tiles.size + a_tiles.size + units[0].size * len(units))
    share = (BLK, blocks * BLK // 4)
    return pl.pallas_call(
        contract_kernel,
        out_shape=[jax.ShapeDtypeStruct(share, jnp.float32)] + [jax.ShapeDtypeStruct(share, jnp.bfloat16)] * 3,
        in_specs=[SMEM, SMEM, SMEM, HBM, HBM] + [HBM] * len(units),
        out_specs=[VMEM] * 4,
        scratch_shapes=[
            pltpu.VMEM((4,) + share, jnp.float32),
            pltpu.SMEM((blocks * slots + 1,), jnp.int32),
            pltpu.VMEM(a_tiles.shape, a_tiles.dtype),
            pltpu.VMEM((2, a_tiles.shape[1] * BLK, 2 * BLK), jnp.bfloat16),
            pltpu.VMEM((2, 2, vectors, BLK, BLK), jnp.bfloat16),
            pltpu.SemaphoreType.DMA,
            pltpu.SemaphoreType.DMA((2, 2)),
            pltpu.SemaphoreType.DMA((2, 2)),
        ],
        compiler_params=pltpu.CompilerParams(vmem_limit_bytes=47 * 1024 * 1024),
        cost_estimate=pl.CostEstimate(flops=flops, bytes_accessed=moved, transcendentals=0),
    )(place, b_source, b_sign, a_tiles, b_tiles, *units)


def gather_sources(place, quarter, a_source, a_sign, alphas):
    zs = alphas // X_SIZE

    def z_from(value, distance):
        return shifted(value, "alpha", alphas, lambda i: (i // X_SIZE - distance) % zs * X_SIZE + i % X_SIZE)

    def x_from(value, distance):
        return shifted(value, "alpha", alphas, lambda i: i // X_SIZE * X_SIZE + (i % X_SIZE - distance) % X_SIZE)

    own = jnp.stack([quarter] + [z_from(quarter, distance) for distance in (1, 2, 3)])
    nxt, prev = x_from(own, 1), x_from(own, 3)
    far_low, far_high = x_from(prev[:2], 3), x_from(nxt[2:], 1)
    slots = a_source.shape[1]
    return pl.pallas_call(
        pick_kernel,
        out_shape=jax.ShapeDtypeStruct((2, slots * BLK, BLK), quarter.dtype),
        in_specs=[SMEM, SMEM, SMEM] + [VMEM] * 5,
        out_specs=VMEM,
        compiler_params=pltpu.CompilerParams(vmem_limit_bytes=8 * 1024 * 1024),
    )(place, a_source, a_sign, own, nxt, prev, far_low, far_high)


def gather_group(unit, betas, chols):
    def y_from(value, distance):
        return shifted(value, "chol", chols, lambda i: (i - distance) % chols)

    def z_other(value):
        return shifted(value, "beta", betas, lambda i: i ^ 2)

    def core_other(value):
        return shifted(value, "beta", betas, lambda i: i ^ 1)

    def onward(i):
        beta, chol = i // chols, i % chols
        return beta * chols + (chol + (1 if beta % 2 == 0 else -1)) % chols

    after, before, across = y_from(unit, 1), y_from(unit, 3), z_other(unit)
    first_core = lax.axis_index("beta") % 2 == 0
    middle = shifted(jnp.where(first_core, before, after), ("beta", "chol"), betas * chols, onward)
    near = [unit, after, middle, before]
    far = [across, y_from(across, 1), z_other(middle), y_from(across, 3)]
    return near + [core_other(v) for v in near] + far + [core_other(v) for v in far]


def per_device(sizes, ci_vector, a_tiles, a_source, a_sign, b_tiles, b_source, b_sign):
    chols = sizes["chol"]
    chol = lax.axis_index("chol")
    place = jnp.stack([lax.axis_index("alpha"), lax.axis_index("beta"), chol]).astype(jnp.int32)
    width = ci_vector.shape[1] // chols
    quarter = lax.dynamic_slice_in_dim(ci_vector, chol * width, width, axis=1)
    unit = gather_sources(place, quarter, a_source, a_sign, sizes["alpha"])
    units = gather_group(unit, sizes["beta"], chols)
    own, *pieces = contract(place, b_source, b_sign, a_tiles[:, 0], b_tiles, units)
    for shift, piece in enumerate(pieces, 1):
        own = own + shifted(piece, "chol", chols, lambda i: (i + shift) % chols).astype(jnp.float32)
    return own.astype(jnp.bfloat16)


def solution(mesh):
    placed = (
        P("alpha", "beta"),
        P("chol", "alpha", None, None, None),
        P("alpha", None),
        P("alpha", None),
        P("chol", "beta", None, None, None),
        P("beta", None),
        P("beta", None),
    )
    sizes = dict(mesh.shape)

    def body(*args):
        return per_device(sizes, *args)

    return jax.shard_map(
        body,
        mesh=mesh,
        in_specs=placed,
        out_specs=P("alpha", ("beta", "chol")),
        check_vma=False,
    )
```

```python
import functools

import jax
import jax.numpy as jnp
from jax import lax
from jax.experimental import pallas as pl
from jax.experimental.pallas import tpu as pltpu
from jax.sharding import PartitionSpec as P

BLK = 128
VECTORS_PER_DOT = 2
VECTORS_PER_GROUP = 4
X_SIZE = 4
A_SLOTS, B_SLOTS, B_BLOCKS = 6, 3, 8
ALPHA, BETA, CHOL, A_SOURCE = 0, 1, 2, 3
A_SIGN = A_SOURCE + A_SLOTS
B_SOURCE = A_SIGN + A_SLOTS
B_SIGN = B_SOURCE + B_SLOTS * B_BLOCKS
ARRIVAL = 0x67532410
SMEM = pl.BlockSpec(memory_space=pltpu.SMEM)
VMEM = pl.BlockSpec(memory_space=pltpu.VMEM)
HBM = pl.BlockSpec(memory_space=pltpu.HBM)


def shifted(value, axis, size, moves_to):
    return lax.ppermute(value, axis, [(i, moves_to(i)) for i in range(size)])


def choose(index, low, high, act):
    if high - low == 1:
        act(low)
        return
    middle = (low + high) // 2

    @pl.when(index < middle)
    def _():
        choose(index, low, middle, act)

    @pl.when(index >= middle)
    def _():
        choose(index, middle, high, act)


def pick_kernel(meta_ref, *refs):
    stacks, out_ref = refs[:X_SIZE], refs[X_SIZE]
    alpha = meta_ref[ALPHA]
    for k in range(A_SLOTS):
        source = meta_ref[A_SOURCE + k]
        sign = meta_ref[A_SIGN + k].astype(jnp.float32).astype(out_ref.dtype)
        dz = ((source >> 2) - (alpha >> 2)) & 3
        dx = (source - alpha) & 3

        def put(i, k=k, sign=sign, dz=dz):
            for half in range(2):
                block = stacks[i][dz, :, half * BLK : (half + 1) * BLK]
                out_ref[half, k * BLK : (k + 1) * BLK, :] = block * sign

        choose(dx, 0, X_SIZE, put)


def contract_kernel(first_unit, count_units, has_sum, last, meta_ref, a_ref, b_ref, *rest):
    units, rest = rest[:count_units], rest[count_units:]
    if has_sum:
        sum_ref, rest = rest[0], rest[1:]
    if last:
        own_ref, *piece_refs = rest[:4]
        acc, rest = rest[4], rest[5:]
    else:
        acc, rest = rest[0], rest[1:]
    tasks, places, c_buf, b_buf, c_sem, b_sem = rest
    pairs = B_BLOCKS * B_SLOTS
    vectors = a_ref.shape[0]
    beta, chol = meta_ref[BETA], meta_ref[CHOL]
    acc[...] = sum_ref[...] if has_sum else jnp.zeros_like(acc)

    count = jnp.int32(0)
    for pair in range(pairs):
        m = meta_ref[B_SOURCE + pair]
        owner = m >> 3
        crossed = owner ^ beta
        dy = ((m >> 1) - chol) & 3
        dy = jnp.where((crossed & 2) * (owner & 1) != 0, (4 - dy) & 3, dy)
        code = (crossed & 2) * 2 + dy
        place = ((jnp.int32(ARRIVAL) >> (4 * code)) & 7) * 2 + (crossed & 1) - first_unit
        tasks[count] = pair
        places[count] = place
        here = (meta_ref[B_SIGN + pair] != 0) & (place >= 0) & (place < count_units)
        count = count + jnp.where(here, 1, 0)
    steps = (count + 1) >> 1

    def index_of(step, half):
        return jnp.minimum(2 * step + half, count - 1)

    def c_copy(unit, m, slot, half):
        return pltpu.make_async_copy(
            unit.at[m & 1], c_buf.at[slot, :, pl.ds(half * BLK, BLK)], c_sem.at[slot, half]
        )

    def b_copy(u, l, slot, half):
        return pltpu.make_async_copy(b_ref.at[:, u, l], b_buf.at[slot, half], b_sem.at[slot, half])

    def start(step, slot):
        for half in range(2):
            at = index_of(step, half)
            pair = tasks[at]
            m = meta_ref[B_SOURCE + pair]
            choose(places[at], 0, count_units, lambda i: c_copy(units[i], m, slot, half).start())
            u = pair // B_SLOTS
            b_copy(u, pair - u * B_SLOTS, slot, half).start()

    @pl.when(steps > 0)
    def _():
        start(0, 0)

    def body(step, carry):
        slot = step & 1

        @pl.when(step + 1 < steps)
        def _():
            start(step + 1, 1 - slot)

        for half in range(2):
            c_copy(units[0], 0, slot, half).wait()
            b_copy(0, 0, slot, half).wait()
        sums = [jnp.zeros((BLK, BLK), jnp.float32) for _ in range(2)]
        for group in range(0, vectors, VECTORS_PER_GROUP):
            panels = []
            for first in range(group, group + VECTORS_PER_GROUP, VECTORS_PER_DOT):
                rows = [
                    jnp.concatenate([a_ref[q, k] for k in range(A_SLOTS)], axis=1)
                    for q in range(first, first + VECTORS_PER_DOT)
                ]
                panel = jnp.dot(
                    jnp.concatenate(rows, axis=0), c_buf[slot], preferred_element_type=jnp.float32
                ).astype(jnp.bfloat16)
                panels += [panel[r * BLK : (r + 1) * BLK] for r in range(VECTORS_PER_DOT)]
            for half in range(2):
                left = [panel[:, half * BLK : (half + 1) * BLK] for panel in panels]
                right = [b_buf[slot, half, group + r] for r in range(VECTORS_PER_GROUP)]
                sums[half] += lax.dot_general(
                    jnp.concatenate(left, axis=1),
                    jnp.concatenate(right, axis=1),
                    (((1,), (1,)), ((), ())),
                    preferred_element_type=jnp.float32,
                )
        for half in range(2):
            pair = tasks[index_of(step, half)]
            live = 2 * step + half < count
            factor = jnp.where(live, meta_ref[B_SIGN + pair], 0).astype(jnp.float32)
            u = pair // B_SLOTS
            lanes = pl.ds(pl.multiple_of((u & 1) * BLK, BLK), BLK)
            acc[u >> 1, :, lanes] += factor * sums[half]
        return carry

    lax.fori_loop(0, steps, body, 0)
    if last:
        own_ref[...] = acc[chol]
        for shift, piece_ref in enumerate(piece_refs, 1):
            piece_ref[...] = acc[(chol + shift) & 3].astype(piece_ref.dtype)


def contract(meta, a_tiles, b_tiles, units, first_unit, running=None, last=False):
    vectors, blocks = b_tiles.shape[:2]
    part = len(units) / 16
    flops = int(part * 2 * (a_tiles.size * blocks * B_SLOTS * BLK + b_tiles.size * BLK))
    moved = int(part * 2 * b_tiles.size) + 2 * a_tiles.size
    share = (BLK, blocks * BLK // 4)
    whole = jax.ShapeDtypeStruct((4,) + share, jnp.float32)
    shares = [jax.ShapeDtypeStruct(share, jnp.float32)] + [jax.ShapeDtypeStruct(share, jnp.bfloat16)] * 3
    sums = [] if running is None else [running]
    return pl.pallas_call(
        functools.partial(contract_kernel, first_unit, len(units), bool(sums), last),
        out_shape=shares if last else whole,
        in_specs=[SMEM, VMEM, HBM] + [HBM] * len(units) + [VMEM] * len(sums),
        out_specs=[VMEM] * 4 if last else VMEM,
        scratch_shapes=[pltpu.VMEM(whole.shape, jnp.float32)] * last
        + [
            pltpu.SMEM((blocks * B_SLOTS + 1,), jnp.int32),
            pltpu.SMEM((blocks * B_SLOTS + 1,), jnp.int32),
            pltpu.VMEM((2, A_SLOTS * BLK, 2 * BLK), jnp.bfloat16),
            pltpu.VMEM((2, 2, vectors, BLK, BLK), jnp.bfloat16),
            pltpu.SemaphoreType.DMA((2, 2)),
            pltpu.SemaphoreType.DMA((2, 2)),
        ],
        compiler_params=pltpu.CompilerParams(vmem_limit_bytes=47 * 1024 * 1024),
        cost_estimate=pl.CostEstimate(flops=flops, bytes_accessed=moved, transcendentals=0),
    )(meta, a_tiles, b_tiles, *units, *sums)


def gather_sources(meta, quarter, sizes):
    alphas, betas = sizes["alpha"], sizes["beta"]
    zs = alphas // X_SIZE

    def x_moved(i, distance):
        return i // X_SIZE * X_SIZE + (i + distance) % X_SIZE

    def z_from(value, distance):
        return shifted(value, "alpha", alphas, lambda i: (i // X_SIZE - distance) % zs * X_SIZE + i % X_SIZE)

    def x_from(value, distance):
        return shifted(value, "alpha", alphas, lambda i: x_moved(i, -distance))

    def onward(i):
        alpha, beta = i // betas, i % betas
        return x_moved(alpha, 1 if beta % 2 == 0 else -1) * betas + beta

    own = jnp.stack([quarter] + [z_from(quarter, distance) for distance in (1, 2, 3)])
    own, meta = lax.optimization_barrier((own, meta))
    after, before = x_from(own, 1), x_from(own, 3)
    first_core = lax.axis_index("beta") % 2 == 0
    far = shifted(jnp.where(first_core, before, after), ("alpha", "beta"), alphas * betas, onward)
    unit = pl.pallas_call(
        pick_kernel,
        out_shape=jax.ShapeDtypeStruct((2, A_SLOTS * BLK, BLK), quarter.dtype),
        in_specs=[SMEM] + [VMEM] * X_SIZE,
        out_specs=VMEM,
        compiler_params=pltpu.CompilerParams(vmem_limit_bytes=8 * 1024 * 1024),
    )(meta, own, after, far, before)
    return meta, unit


def gather_and_contract(meta, unit, a_tiles, b_tiles, sizes):
    betas, chols = sizes["beta"], sizes["chol"]

    def y_from(value, distance):
        return shifted(value, "chol", chols, lambda i: (i - distance) % chols)

    def z_other(value):
        return shifted(value, "beta", betas, lambda i: i ^ 2)

    def both(values):
        return [v for value in values for v in (value, shifted(value, "beta", betas, lambda i: i ^ 1))]

    def by_core(value, sense):
        def moved(i):
            beta, chol = i // chols, i % chols
            return beta * chols + (chol + (sense if beta % 2 == 0 else -sense)) % chols

        return shifted(value, ("beta", "chol"), betas * chols, moved)

    after, before, across = y_from(unit, 1), y_from(unit, 3), z_other(unit)
    onward = jnp.where(lax.axis_index("beta") % 2 == 0, before, after)
    middle, far_onward, far_back = by_core(onward, 1), z_other(onward), by_core(across, -1)
    first = both([unit, after, before, across])
    running = contract(meta, a_tiles, b_tiles, first, 0)
    running, middle, far_back, far_onward = lax.optimization_barrier((running, middle, far_back, far_onward))
    far_middle = by_core(far_onward, 1)
    second = both([middle, far_back, far_onward])
    running = contract(meta, a_tiles, b_tiles, second, 8, running)
    running, far_middle = lax.optimization_barrier((running, far_middle))
    return contract(meta, a_tiles, b_tiles, both([far_middle]), 14, running, last=True)


def per_device(sizes, ci_vector, a_tiles, a_source, a_sign, b_tiles, b_source, b_sign):
    chols = sizes["chol"]
    chol = lax.axis_index("chol")
    place = jnp.stack([lax.axis_index("alpha"), lax.axis_index("beta"), chol]).astype(jnp.int32)
    meta = jnp.concatenate([place] + [v.reshape(-1) for v in (a_source, a_sign, b_source, b_sign)])
    width = ci_vector.shape[1] // chols
    quarter = lax.dynamic_slice_in_dim(ci_vector, chol * width, width, axis=1)
    meta, unit = gather_sources(meta, quarter, sizes)
    own, *pieces = gather_and_contract(meta, unit, a_tiles[:, 0], b_tiles, sizes)
    for shift, piece in enumerate(pieces, 1):
        own = own + shifted(piece, "chol", chols, lambda i: (i + shift) % chols).astype(jnp.float32)
    return own.astype(jnp.bfloat16)


def solution(mesh):
    placed = (
        P("alpha", "beta"),
        P("chol", "alpha", None, None, None),
        P("alpha", None),
        P("alpha", None),
        P("chol", "beta", None, None, None),
        P("beta", None),
        P("beta", None),
    )
    sizes = dict(mesh.shape)

    def body(*args):
        return per_device(sizes, *args)

    return jax.shard_map(
        body,
        mesh=mesh,
        in_specs=placed,
        out_specs=P("alpha", ("beta", "chol")),
        check_vma=False,
    )
```

```python
import functools

import jax
import jax.numpy as jnp
from jax import lax
from jax.experimental import pallas as pl
from jax.experimental.pallas import tpu as pltpu
from jax.sharding import PartitionSpec as P

BLK = 128
VECTORS_PER_GROUP = 4
WIDE, NARROW = 4, 2
X_SIZE = 4
A_SLOTS, B_SLOTS, B_BLOCKS = 6, 3, 8
ALPHA, BETA, CHOL, A_SOURCE = 0, 1, 2, 3
A_SIGN = A_SOURCE + A_SLOTS
B_SOURCE = A_SIGN + A_SLOTS
B_SIGN = B_SOURCE + B_SLOTS * B_BLOCKS
ARRIVAL = 0x67532410
SMEM = pl.BlockSpec(memory_space=pltpu.SMEM)
VMEM = pl.BlockSpec(memory_space=pltpu.VMEM)
HBM = pl.BlockSpec(memory_space=pltpu.HBM)


def shifted(value, axis, size, moves_to):
    return lax.ppermute(value, axis, [(i, moves_to(i)) for i in range(size)])


def choose(index, low, high, act):
    if high - low == 1:
        act(low)
        return
    middle = (low + high) // 2

    @pl.when(index < middle)
    def _():
        choose(index, low, middle, act)

    @pl.when(index >= middle)
    def _():
        choose(index, middle, high, act)


def flip_kernel(a_ref, out_ref):
    for q in range(a_ref.shape[0]):
        for k in range(A_SLOTS):
            out_ref[k * BLK : (k + 1) * BLK, q * BLK : (q + 1) * BLK] = a_ref[q, 0, k].T


def pick_kernel(meta_ref, own_ref, after_ref, before_ref, far_low_ref, far_high_ref, out_ref):
    alpha = meta_ref[ALPHA]
    for k in range(A_SLOTS):
        source = meta_ref[A_SOURCE + k]
        sign = meta_ref[A_SIGN + k].astype(jnp.float32).astype(out_ref.dtype)
        dz = ((source >> 2) - (alpha >> 2)) & 3
        dx = (source - alpha) & 3

        def put(ref, at, k=k, sign=sign):
            for half in range(2):
                block = ref[at, :, half * BLK : (half + 1) * BLK]
                out_ref[half, :, k * BLK : (k + 1) * BLK] = block.T * sign

        for distance, ref in ((0, own_ref), (1, after_ref), (3, before_ref)):

            @pl.when(dx == distance)
            def _(ref=ref, put=put, dz=dz):
                put(ref, dz)

        @pl.when((dx == 2) & (dz < 2))
        def _(put=put, dz=dz):
            put(far_low_ref, jnp.minimum(dz, 1))

        @pl.when((dx == 2) & (dz >= 2))
        def _(put=put, dz=dz):
            put(far_high_ref, jnp.maximum(dz - 2, 0))


def contract_kernel(first_unit, count_units, has_sum, last, meta_ref, a_ref, b_ref, *rest):
    units, rest = rest[:count_units], rest[count_units:]
    if has_sum:
        sum_ref, rest = rest[0], rest[1:]
    if last:
        own_ref, *piece_refs = rest[:4]
        acc, rest = rest[4], rest[5:]
    else:
        acc, rest = rest[0], rest[1:]
    tasks, places, c_buf, b_buf, c_sem, b_sem = rest
    pairs = B_BLOCKS * B_SLOTS
    vectors = b_ref.shape[0]
    beta, chol = meta_ref[BETA], meta_ref[CHOL]
    acc[...] = sum_ref[...] if has_sum else jnp.zeros_like(acc)

    count = jnp.int32(0)
    for pair in range(pairs):
        m = meta_ref[B_SOURCE + pair]
        owner = m >> 3
        crossed = owner ^ beta
        dy = ((m >> 1) - chol) & 3
        dy = jnp.where((crossed & 2) * (owner & 1) != 0, (4 - dy) & 3, dy)
        code = (crossed & 2) * 2 + dy
        place = ((jnp.int32(ARRIVAL) >> (4 * code)) & 7) * 2 + (crossed & 1) - first_unit
        tasks[count] = pair
        places[count] = place
        here = (meta_ref[B_SIGN + pair] != 0) & (place >= 0) & (place < count_units)
        count = count + jnp.where(here, 1, 0)
    wide_steps = count >> 2
    narrow_steps = (count - WIDE * wide_steps + 1) >> 1
    steps = wide_steps + narrow_steps

    def first_of(step):
        return jnp.where(step < wide_steps, WIDE * step, NARROW * step + (WIDE - NARROW) * wide_steps)

    def c_copy(unit, m, slot, lane):
        return pltpu.make_async_copy(
            unit.at[m & 1], c_buf.at[slot, pl.ds(lane * BLK, BLK)], c_sem.at[slot, lane]
        )

    def b_copy(u, l, slot, lane):
        return pltpu.make_async_copy(b_ref.at[:, u, l], b_buf.at[slot, lane], b_sem.at[slot, lane])

    def start(step, slot, lanes):
        for lane in lanes:
            at = jnp.minimum(first_of(step) + lane, count - 1)
            pair = tasks[at]
            m = meta_ref[B_SOURCE + pair]
            choose(places[at], 0, count_units, lambda i: c_copy(units[i], m, slot, lane).start())
            u = pair // B_SLOTS
            b_copy(u, pair - u * B_SLOTS, slot, lane).start()

    def start_step(step, slot):
        @pl.when(step < steps)
        def _():
            start(step, slot, range(NARROW))

        @pl.when(step < wide_steps)
        def _():
            start(step, slot, range(NARROW, WIDE))

    start_step(0, 0)

    def body(width, step, carry):
        slot = step & 1
        start_step(step + 1, 1 - slot)
        for lane in range(width):
            c_copy(units[0], 0, slot, lane).wait()
            b_copy(0, 0, slot, lane).wait()
        sums = [jnp.zeros((BLK, BLK), jnp.float32) for _ in range(width)]
        for group in range(0, vectors, VECTORS_PER_GROUP):
            columns = slice(group * BLK, (group + VECTORS_PER_GROUP) * BLK)
            panel = jnp.dot(
                c_buf[slot, : width * BLK], a_ref[:, columns], preferred_element_type=jnp.float32
            ).astype(jnp.bfloat16)
            for lane in range(width):
                tiles = [b_buf[slot, lane, group + r] for r in range(VECTORS_PER_GROUP)]
                blocks = [
                    panel[lane * BLK : (lane + 1) * BLK, r * BLK : (r + 1) * BLK]
                    for r in range(VECTORS_PER_GROUP)
                ]
                sums[lane] += jnp.dot(
                    jnp.concatenate(tiles, axis=1),
                    jnp.concatenate(blocks, axis=0),
                    preferred_element_type=jnp.float32,
                )
        for lane in range(width):
            at = first_of(step) + lane
            pair = tasks[jnp.minimum(at, count - 1)]
            factor = jnp.where(at < count, meta_ref[B_SIGN + pair], 0).astype(jnp.float32)
            acc[pair // B_SLOTS] += factor * sums[lane]
        return carry

    lax.fori_loop(0, wide_steps, functools.partial(body, WIDE), 0)
    lax.fori_loop(wide_steps, steps, functools.partial(body, NARROW), 0)
    if last:
        for shift, out_ref in enumerate([own_ref] + piece_refs):
            for half in range(2):
                block = acc[((chol + shift) & 3) * 2 + half].T
                out_ref[:, half * BLK : (half + 1) * BLK] = block.astype(out_ref.dtype)


def contract(meta, a_flipped, b_tiles, units, first_unit, running=None, last=False):
    vectors, blocks = b_tiles.shape[:2]
    part = len(units) / 16
    flops = int(part * 2 * (a_flipped.size * blocks * B_SLOTS * BLK + b_tiles.size * BLK))
    moved = int(part * 2 * b_tiles.size) + 2 * a_flipped.size
    share = (BLK, blocks * BLK // 4)
    whole = jax.ShapeDtypeStruct((blocks, BLK, BLK), jnp.float32)
    shares = [jax.ShapeDtypeStruct(share, jnp.float32)] + [jax.ShapeDtypeStruct(share, jnp.bfloat16)] * 3
    sums = [] if running is None else [running]
    return pl.pallas_call(
        functools.partial(contract_kernel, first_unit, len(units), bool(sums), last),
        out_shape=shares if last else whole,
        in_specs=[SMEM, VMEM, HBM] + [HBM] * len(units) + [VMEM] * len(sums),
        out_specs=[VMEM] * 4 if last else VMEM,
        scratch_shapes=[pltpu.VMEM(whole.shape, jnp.float32)] * last
        + [
            pltpu.SMEM((blocks * B_SLOTS + 1,), jnp.int32),
            pltpu.SMEM((blocks * B_SLOTS + 1,), jnp.int32),
            pltpu.VMEM((2, WIDE * BLK, A_SLOTS * BLK), jnp.bfloat16),
            pltpu.VMEM((2, WIDE, vectors, BLK, BLK), jnp.bfloat16),
            pltpu.SemaphoreType.DMA((2, WIDE)),
            pltpu.SemaphoreType.DMA((2, WIDE)),
        ],
        compiler_params=pltpu.CompilerParams(vmem_limit_bytes=47 * 1024 * 1024),
        cost_estimate=pl.CostEstimate(flops=flops, bytes_accessed=moved, transcendentals=0),
    )(meta, a_flipped, b_tiles, *units, *sums)


def flip(a_tiles):
    vectors = a_tiles.shape[0]
    return pl.pallas_call(
        flip_kernel,
        out_shape=jax.ShapeDtypeStruct((A_SLOTS * BLK, vectors * BLK), a_tiles.dtype),
        in_specs=[VMEM],
        out_specs=VMEM,
        compiler_params=pltpu.CompilerParams(vmem_limit_bytes=16 * 1024 * 1024),
        cost_estimate=pl.CostEstimate(flops=0, bytes_accessed=4 * a_tiles.size, transcendentals=0),
    )(a_tiles)


def gather_sources(meta, quarter, a_tiles, alphas):
    zs = alphas // X_SIZE

    def z_from(value, distance):
        return shifted(value, "alpha", alphas, lambda i: (i // X_SIZE - distance) % zs * X_SIZE + i % X_SIZE)

    def x_from(value, distance):
        return shifted(value, "alpha", alphas, lambda i: i // X_SIZE * X_SIZE + (i % X_SIZE - distance) % X_SIZE)

    own = jnp.stack([quarter] + [z_from(quarter, distance) for distance in (1, 2, 3)])
    after, before = x_from(own, 1), x_from(own, 3)
    after, meta, a_flipped = lax.optimization_barrier((after, meta, flip(a_tiles)))
    far_low, far_high = x_from(before[:2], 3), x_from(after[2:], 1)
    unit = pl.pallas_call(
        pick_kernel,
        out_shape=jax.ShapeDtypeStruct((2, BLK, A_SLOTS * BLK), quarter.dtype),
        in_specs=[SMEM] + [VMEM] * 5,
        out_specs=VMEM,
        compiler_params=pltpu.CompilerParams(vmem_limit_bytes=8 * 1024 * 1024),
    )(meta, own, after, before, far_low, far_high)
    return meta, unit, a_flipped


def gather_and_contract(meta, unit, a_flipped, b_tiles, sizes):
    betas, chols = sizes["beta"], sizes["chol"]

    def y_from(value, distance):
        return shifted(value, "chol", chols, lambda i: (i - distance) % chols)

    def z_other(value):
        return shifted(value, "beta", betas, lambda i: i ^ 2)

    def both(values):
        return [v for value in values for v in (value, shifted(value, "beta", betas, lambda i: i ^ 1))]

    def by_core(value, sense):
        def moved(i):
            beta, chol = i // chols, i % chols
            return beta * chols + (chol + (sense if beta % 2 == 0 else -sense)) % chols

        return shifted(value, ("beta", "chol"), betas * chols, moved)

    after, before, across = y_from(unit, 1), y_from(unit, 3), z_other(unit)
    onward = jnp.where(lax.axis_index("beta") % 2 == 0, before, after)
    middle, far_onward, far_back = by_core(onward, 1), z_other(onward), by_core(across, -1)
    first = both([unit, after, before, across])
    running = contract(meta, a_flipped, b_tiles, first, 0)
    running, middle, far_back, far_onward = lax.optimization_barrier((running, middle, far_back, far_onward))
    far_middle = by_core(far_onward, 1)
    second = both([middle, far_back, far_onward])
    running = contract(meta, a_flipped, b_tiles, second, 8, running)
    running, far_middle = lax.optimization_barrier((running, far_middle))
    return contract(meta, a_flipped, b_tiles, both([far_middle]), 14, running, last=True)


def per_device(sizes, ci_vector, a_tiles, a_source, a_sign, b_tiles, b_source, b_sign):
    chols = sizes["chol"]
    chol = lax.axis_index("chol")
    place = jnp.stack([lax.axis_index("alpha"), lax.axis_index("beta"), chol]).astype(jnp.int32)
    meta = jnp.concatenate([place] + [v.reshape(-1) for v in (a_source, a_sign, b_source, b_sign)])
    width = ci_vector.shape[1] // chols
    quarter = lax.dynamic_slice_in_dim(ci_vector, chol * width, width, axis=1)
    meta, unit, a_flipped = gather_sources(meta, quarter, a_tiles, sizes["alpha"])
    own, *pieces = gather_and_contract(meta, unit, a_flipped, b_tiles, sizes)
    for shift, piece in enumerate(pieces, 1):
        own = own + shifted(piece, "chol", chols, lambda i: (i + shift) % chols).astype(jnp.float32)
    return own.astype(jnp.bfloat16)


def solution(mesh):
    placed = (
        P("alpha", "beta"),
        P("chol", "alpha", None, None, None),
        P("alpha", None),
        P("alpha", None),
        P("chol", "beta", None, None, None),
        P("beta", None),
        P("beta", None),
    )
    sizes = dict(mesh.shape)

    def body(*args):
        return per_device(sizes, *args)

    return jax.shard_map(
        body,
        mesh=mesh,
        in_specs=placed,
        out_specs=P("alpha", ("beta", "chol")),
        check_vma=False,
    )
```

```python
import functools

import jax
import jax.numpy as jnp
from jax import lax
from jax.experimental import pallas as pl
from jax.experimental.pallas import tpu as pltpu
from jax.sharding import PartitionSpec as P

BLK = 128
VECTORS_PER_GROUP = 4
WIDE, NARROW = 4, 2
X_SIZE = 4
A_SLOTS, B_SLOTS, B_BLOCKS = 6, 3, 8
PAIRS = B_SLOTS * B_BLOCKS
ALPHA, BETA, CHOL, A_SOURCE = 0, 1, 2, 3
A_SIGN = A_SOURCE + A_SLOTS
B_SOURCE = A_SIGN + A_SLOTS
B_SIGN = B_SOURCE + PAIRS
OTHER = 2 * PAIRS
ARRIVAL = 0x67521430
FIRST_UNITS = (0, 1, 4, 7, 8)
KERNELS = len(FIRST_UNITS) - 1
PLAN = 64
SMEM = pl.BlockSpec(memory_space=pltpu.SMEM)
VMEM = pl.BlockSpec(memory_space=pltpu.VMEM)
HBM = pl.BlockSpec(memory_space=pltpu.HBM)


def shifted(value, axis, size, moves_to):
    return lax.ppermute(value, axis, [(i, moves_to(i)) for i in range(size)])


def choose(index, low, high, act):
    if high - low == 1:
        act(low)
        return
    middle = (low + high) // 2

    @pl.when(index < middle)
    def _():
        choose(index, low, middle, act)

    @pl.when(index >= middle)
    def _():
        choose(index, middle, high, act)


def flip_kernel(a_hbm, out_ref, a_buf, sems):
    parts = sems.shape[0]
    size = a_buf.shape[0] // parts
    copies = [
        pltpu.make_async_copy(a_hbm.at[pl.ds(p * size, size)], a_buf.at[pl.ds(p * size, size)], sems.at[p])
        for p in range(parts)
    ]
    for copy in copies:
        copy.start()
    for p, copy in enumerate(copies):
        copy.wait()
        for q in range(p * size, (p + 1) * size):
            for k in range(A_SLOTS):
                out_ref[k * BLK : (k + 1) * BLK, q * BLK : (q + 1) * BLK] = a_buf[q, 0, k].T


def plan_kernel(meta_ref, plan_ref):
    beta, chol = meta_ref[BETA], meta_ref[CHOL]
    core = beta & 1
    counts = [jnp.int32(0)] * KERNELS
    for pair in range(2 * PAIRS):
        base = OTHER if pair >= PAIRS else 0
        m = meta_ref[B_SOURCE + base + pair % PAIRS]
        sign = meta_ref[B_SIGN + base + pair % PAIRS]
        owner = m >> 3
        dy = ((m >> 1) - chol) & 3
        dy = jnp.where(core != 0, (4 - dy) & 3, dy)
        unit = (jnp.int32(ARRIVAL) >> (4 * (((owner ^ beta) & 2) * 2 + dy))) & 7
        live = (sign != 0) & ((owner & 1) == core)
        for index in range(KERNELS):
            low, high = FIRST_UNITS[index], FIRST_UNITS[index + 1]
            entry = pair + ((unit - low) << 6) + ((m & 1) << 9) + ((sign + 1) << 10)
            plan_ref[index * PLAN + 1 + counts[index]] = entry
            counts[index] = counts[index] + jnp.where(live & (unit >= low) & (unit < high), 1, 0)
    for index in range(KERNELS):
        plan_ref[index * PLAN] = counts[index]


def pick_kernel(meta_ref, own_ref, back_ref, far_ref, ahead_ref, out_ref):
    alpha = meta_ref[ALPHA]
    core = meta_ref[BETA] & 1
    for k in range(A_SLOTS):
        source = meta_ref[A_SOURCE + k]
        sign = meta_ref[A_SIGN + k].astype(jnp.float32).astype(out_ref.dtype)
        dz = ((source >> 2) - (alpha >> 2)) & 3
        dx = (source - alpha) & 3
        dx = jnp.where(core != 0, (4 - dx) & 3, dx)

        def put(i, k=k, sign=sign, dz=dz):
            for half in range(2):
                block = (own_ref, back_ref, far_ref, ahead_ref)[i][dz, :, half * BLK : (half + 1) * BLK]
                out_ref[half, :, k * BLK : (k + 1) * BLK] = block.T * sign

        choose(dx, 0, X_SIZE, put)


def contract_kernel(index, last, plan_ref, a_ref, b_own, b_other, *rest):
    count_units = FIRST_UNITS[index + 1] - FIRST_UNITS[index]
    units, rest = rest[:count_units], rest[count_units:]
    if index:
        sum_ref, rest = rest[0], rest[1:]
    if last:
        chol_ref, mine_ref, other_ref, acc, c_buf, b_buf, c_sem, b_sem = rest
    else:
        acc, c_buf, b_buf, c_sem, b_sem = rest
    vectors = b_own.shape[0]
    count = plan_ref[index * PLAN]
    wide_steps = count >> 2
    narrow_steps = (count - WIDE * wide_steps + 1) >> 1
    steps = wide_steps + narrow_steps

    def first_of(step):
        return jnp.where(step < wide_steps, WIDE * step, NARROW * step + (WIDE - NARROW) * wide_steps)

    def entry_of(at):
        return plan_ref[index * PLAN + 1 + jnp.minimum(at, count - 1)]

    def c_copy(unit, half, slot, lane):
        return pltpu.make_async_copy(
            unit.at[half], c_buf.at[slot, pl.ds(lane * BLK, BLK)], c_sem.at[slot, lane]
        )

    def b_copy(ref, u, l, slot, lane, part):
        vectors_of = (pl.ds(0, VECTORS_PER_GROUP), pl.ds(VECTORS_PER_GROUP, vectors - VECTORS_PER_GROUP))[part]
        return pltpu.make_async_copy(
            ref.at[vectors_of, u, l], b_buf.at[slot, lane, vectors_of], b_sem.at[slot, lane, part]
        )

    def start_c(step, slot, lanes):
        for lane in lanes:
            entry = entry_of(first_of(step) + lane)
            half = (entry >> 9) & 1
            choose((entry >> 6) & 7, 0, count_units, lambda i: c_copy(units[i], half, slot, lane).start())

    def start_b(step, slot, lanes, part):
        for lane in lanes:
            entry = entry_of(first_of(step) + lane)
            pair = entry & 63
            foreign = pair >= PAIRS
            pair = jnp.where(foreign, pair - PAIRS, pair)
            u = pair // B_SLOTS
            l = pair - u * B_SLOTS

            @pl.when(foreign)
            def _(u=u, l=l, lane=lane):
                b_copy(b_other, u, l, slot, lane, part).start()

            @pl.when(jnp.logical_not(foreign))
            def _(u=u, l=l, lane=lane):
                b_copy(b_own, u, l, slot, lane, part).start()

    def start_step(step, slot):
        def start(lanes):
            start_c(step, slot, lanes)
            for part in range(2):
                start_b(step, slot, lanes, part)

        @pl.when(step < wide_steps)
        def _():
            start(range(WIDE))

        @pl.when((step >= wide_steps) & (step < steps))
        def _():
            start(range(NARROW))

    start_step(0, 0)
    acc[...] = sum_ref[...] if index else jnp.zeros_like(acc)

    def body(width, step, carry):
        slot = step & 1
        start_step(step + 1, 1 - slot)
        for lane in range(width):
            c_copy(units[0], 0, slot, lane).wait()
        sums = [jnp.zeros((BLK, BLK), jnp.float32) for _ in range(width)]
        for group in range(0, vectors, VECTORS_PER_GROUP):
            columns = slice(group * BLK, (group + VECTORS_PER_GROUP) * BLK)
            panel = jnp.dot(
                c_buf[slot, : width * BLK], a_ref[:, columns], preferred_element_type=jnp.float32
            ).astype(jnp.bfloat16)
            if group <= VECTORS_PER_GROUP:
                for lane in range(width):
                    b_copy(b_own, 0, 0, slot, lane, group // VECTORS_PER_GROUP).wait()
            for lane in range(width):
                tiles = [b_buf[slot, lane, group + r] for r in range(VECTORS_PER_GROUP)]
                blocks = [
                    panel[lane * BLK : (lane + 1) * BLK, r * BLK : (r + 1) * BLK]
                    for r in range(VECTORS_PER_GROUP)
                ]
                sums[lane] += jnp.dot(
                    jnp.concatenate(tiles, axis=1),
                    jnp.concatenate(blocks, axis=0),
                    preferred_element_type=jnp.float32,
                )
        for lane in range(width):
            at = first_of(step) + lane
            entry = entry_of(at)
            factor = jnp.where(at < count, (entry >> 10) - 1, 0).astype(jnp.float32)
            acc[(entry & 63) // B_SLOTS] += factor * sums[lane]
        return carry

    lax.fori_loop(0, wide_steps, functools.partial(body, WIDE), 0)
    lax.fori_loop(wide_steps, steps, functools.partial(body, NARROW), 0)
    if last:
        for shift in range(4):
            for half in range(2):
                u = ((chol_ref[0] + shift) & 3) * 2 + half
                lanes = slice(half * BLK, (half + 1) * BLK)
                mine_ref[shift, :, lanes] = acc[u].T
                other_ref[shift, :, lanes] = acc[B_BLOCKS + u].T


def contract(index, plan, a_flipped, b_own, b_other, units, running=None, chol=None):
    vectors, blocks = b_own.shape[:2]
    last = chol is not None
    part = len(units) / 8
    flops = int(part * 2 * (a_flipped.size * blocks * B_SLOTS * BLK + b_own.size * BLK))
    moved = int(part * 2 * b_own.size) + 2 * a_flipped.size
    whole = jax.ShapeDtypeStruct((2 * blocks, BLK, BLK), jnp.float32)
    shares = jax.ShapeDtypeStruct((4, BLK, blocks * BLK // 4), jnp.float32)
    sums = [] if running is None else [running]
    chols = [chol] if last else []
    return pl.pallas_call(
        functools.partial(contract_kernel, index, last),
        out_shape=[shares, shares] if last else whole,
        in_specs=[SMEM, VMEM, HBM, HBM] + [HBM] * len(units) + [VMEM] * len(sums) + [SMEM] * len(chols),
        out_specs=[VMEM, VMEM] if last else VMEM,
        scratch_shapes=[pltpu.VMEM(whole.shape, jnp.float32)] * last
        + [
            pltpu.VMEM((2, WIDE * BLK, A_SLOTS * BLK), jnp.bfloat16),
            pltpu.VMEM((2, WIDE, vectors, BLK, BLK), jnp.bfloat16),
            pltpu.SemaphoreType.DMA((2, WIDE)),
            pltpu.SemaphoreType.DMA((2, WIDE, 2)),
        ],
        compiler_params=pltpu.CompilerParams(vmem_limit_bytes=47 * 1024 * 1024),
        cost_estimate=pl.CostEstimate(flops=flops, bytes_accessed=moved, transcendentals=0),
    )(plan, a_flipped, b_own, b_other, *units, *sums, *chols)


def merge_kernel(mine_ref, arrived_ref, own_ref, *piece_refs):
    own_ref[...] = mine_ref[0] + arrived_ref[0]
    for shift, piece_ref in enumerate(piece_refs, 1):
        piece_ref[...] = (mine_ref[shift] + arrived_ref[shift]).astype(piece_ref.dtype)


def merge(mine, arrived):
    shape = mine.shape[1:]
    return pl.pallas_call(
        merge_kernel,
        out_shape=[jax.ShapeDtypeStruct(shape, jnp.float32)] + [jax.ShapeDtypeStruct(shape, jnp.bfloat16)] * 3,
        in_specs=[VMEM, VMEM],
        out_specs=[VMEM] * 4,
        compiler_params=pltpu.CompilerParams(vmem_limit_bytes=8 * 1024 * 1024),
    )(mine, arrived)


def flip(a_tiles):
    vectors = a_tiles.shape[0]
    return pl.pallas_call(
        flip_kernel,
        out_shape=jax.ShapeDtypeStruct((A_SLOTS * BLK, vectors * BLK), a_tiles.dtype),
        in_specs=[HBM],
        out_specs=VMEM,
        scratch_shapes=[pltpu.VMEM(a_tiles.shape, a_tiles.dtype), pltpu.SemaphoreType.DMA((4,))],
        compiler_params=pltpu.CompilerParams(vmem_limit_bytes=48 * 1024 * 1024),
        cost_estimate=pl.CostEstimate(flops=0, bytes_accessed=4 * a_tiles.size, transcendentals=0),
    )(a_tiles)


def make_plan(meta):
    return pl.pallas_call(
        plan_kernel,
        out_shape=jax.ShapeDtypeStruct((KERNELS * PLAN,), jnp.int32),
        in_specs=[SMEM],
        out_specs=SMEM,
    )(meta)


def gather_sources(meta, quarter, sizes):
    alphas, betas = sizes["alpha"], sizes["beta"]
    zs = alphas // X_SIZE

    def z_from(value, distance):
        return shifted(value, "alpha", alphas, lambda i: (i // X_SIZE - distance) % zs * X_SIZE + i % X_SIZE)

    def by_core(value, sense):
        def moved(i):
            alpha, beta = i // betas, i % betas
            x = (alpha + (sense if beta % 2 == 0 else -sense)) % X_SIZE
            return (alpha // X_SIZE * X_SIZE + x) * betas + beta

        return shifted(value, ("alpha", "beta"), alphas * betas, moved)

    others = [z_from(quarter, distance) for distance in (1, 2, 3)]
    others[1], meta = lax.optimization_barrier((others[1], meta))
    own = jnp.stack([quarter] + others)
    ahead, back = by_core(own, 1), by_core(own, -1)
    ahead, plan = lax.optimization_barrier((ahead, make_plan(meta)))
    far = by_core(ahead, 1)
    unit = pl.pallas_call(
        pick_kernel,
        out_shape=jax.ShapeDtypeStruct((2, BLK, A_SLOTS * BLK), quarter.dtype),
        in_specs=[SMEM] + [VMEM] * 4,
        out_specs=VMEM,
        compiler_params=pltpu.CompilerParams(vmem_limit_bytes=8 * 1024 * 1024),
    )(meta, own, back, far, ahead)
    return plan, unit


def gather_and_contract(plan, chol, unit, a_tiles, b_own, b_other, sizes):
    betas, chols = sizes["beta"], sizes["chol"]

    def z_other(value):
        return shifted(value, "beta", betas, lambda i: i ^ 2)

    def by_core(value, sense):
        def moved(i):
            beta, chol = i // chols, i % chols
            return beta * chols + (chol + (sense if beta % 2 == 0 else -sense)) % chols

        return shifted(value, ("beta", "chol"), betas * chols, moved)

    ahead, across, back = by_core(unit, 1), z_other(unit), by_core(unit, -1)
    tiles = (plan, flip(a_tiles), b_own, b_other)
    running = contract(0, *tiles, [unit])
    running, ahead, across, back = lax.optimization_barrier((running, ahead, across, back))
    middle, far_ahead, far_back = by_core(ahead, 1), z_other(ahead), by_core(across, -1)
    running = contract(1, *tiles, [ahead, across, back], running)
    running, middle, far_back, far_ahead = lax.optimization_barrier((running, middle, far_back, far_ahead))
    far_middle = by_core(far_ahead, 1)
    running = contract(2, *tiles, [middle, far_back, far_ahead], running)
    running, far_middle = lax.optimization_barrier((running, far_middle))
    return contract(3, *tiles, [far_middle], running, chol=chol)


def per_device(sizes, ci_vector, a_tiles, a_source, a_sign, b_tiles, b_source, b_sign):
    betas, chols = sizes["beta"], sizes["chol"]

    def core_other(value):
        return shifted(value, "beta", betas, lambda i: i ^ 1)

    chol = lax.axis_index("chol").astype(jnp.int32)
    width = ci_vector.shape[1] // chols
    quarter = lax.dynamic_slice_in_dim(ci_vector, chol * width, width, axis=1)
    place = jnp.stack([lax.axis_index("alpha"), lax.axis_index("beta"), chol]).astype(jnp.int32)
    pairs = jnp.concatenate([b_source.reshape(-1), b_sign.reshape(-1)])
    meta = jnp.concatenate([place, a_source.reshape(-1), a_sign.reshape(-1), pairs, core_other(pairs)])
    plan, unit = gather_sources(meta, quarter, sizes)
    mine, other = gather_and_contract(plan, chol[None], unit, a_tiles, b_tiles, core_other(b_tiles), sizes)
    own, *pieces = merge(mine, core_other(other))
    for shift, piece in enumerate(pieces, 1):
        own = own + shifted(piece, "chol", chols, lambda i: (i + shift) % chols).astype(jnp.float32)
    return own.astype(jnp.bfloat16)


def solution(mesh):
    placed = (
        P("alpha", "beta"),
        P("chol", "alpha", None, None, None),
        P("alpha", None),
        P("alpha", None),
        P("chol", "beta", None, None, None),
        P("beta", None),
        P("beta", None),
    )
    sizes = dict(mesh.shape)

    def body(*args):
        return per_device(sizes, *args)

    return jax.shard_map(
        body,
        mesh=mesh,
        in_specs=placed,
        out_specs=P("alpha", ("beta", "chol")),
        check_vma=False,
    )
```

```python
import functools

import jax
import jax.numpy as jnp
from jax import lax
from jax.experimental import pallas as pl
from jax.experimental.pallas import tpu as pltpu
from jax.sharding import PartitionSpec as P

BLK = 128
VECTORS_PER_GROUP = 4
WIDE, NARROW = 4, 2
X_SIZE = 4
A_SLOTS, B_SLOTS, B_BLOCKS = 6, 3, 8
PAIRS = B_SLOTS * B_BLOCKS
ALPHA, BETA, CHOL, A_SOURCE = 0, 1, 2, 3
A_SIGN = A_SOURCE + A_SLOTS
B_SOURCE = A_SIGN + A_SLOTS
B_SIGN = B_SOURCE + PAIRS
OTHER = 2 * PAIRS
ARRIVAL = 0x67521430
FIRST_UNITS = (0, 1, 4, 7, 8)
KERNELS = len(FIRST_UNITS) - 1
PLAN = 64
SMEM = pl.BlockSpec(memory_space=pltpu.SMEM)
VMEM = pl.BlockSpec(memory_space=pltpu.VMEM)
HBM = pl.BlockSpec(memory_space=pltpu.HBM)


def shifted(value, axis, size, moves_to):
    return lax.ppermute(value, axis, [(i, moves_to(i)) for i in range(size)])


def choose(index, low, high, act):
    if high - low == 1:
        act(low)
        return
    middle = (low + high) // 2

    @pl.when(index < middle)
    def _():
        choose(index, low, middle, act)

    @pl.when(index >= middle)
    def _():
        choose(index, middle, high, act)


def flip_kernel(a_hbm, out_ref, a_buf, sems):
    parts = sems.shape[0]
    size = a_buf.shape[0] // parts
    copies = [
        pltpu.make_async_copy(a_hbm.at[pl.ds(p * size, size)], a_buf.at[pl.ds(p * size, size)], sems.at[p])
        for p in range(parts)
    ]
    for copy in copies:
        copy.start()
    for p, copy in enumerate(copies):
        copy.wait()
        for q in range(p * size, (p + 1) * size):
            for k in range(A_SLOTS):
                out_ref[k * BLK : (k + 1) * BLK, q * BLK : (q + 1) * BLK] = a_buf[q, 0, k].T


def plan_kernel(meta_ref, plan_ref):
    beta, chol = meta_ref[BETA], meta_ref[CHOL]
    core = beta & 1
    counts = [jnp.int32(0)] * KERNELS
    for pair in range(2 * PAIRS):
        base = OTHER if pair >= PAIRS else 0
        m = meta_ref[B_SOURCE + base + pair % PAIRS]
        sign = meta_ref[B_SIGN + base + pair % PAIRS]
        owner = m >> 3
        dy = ((m >> 1) - chol) & 3
        dy = jnp.where(core != 0, (4 - dy) & 3, dy)
        unit = (jnp.int32(ARRIVAL) >> (4 * (((owner ^ beta) & 2) * 2 + dy))) & 7
        live = (sign != 0) & ((owner & 1) == core)
        for index in range(KERNELS):
            low, high = FIRST_UNITS[index], FIRST_UNITS[index + 1]
            entry = pair + ((unit - low) << 6) + ((m & 1) << 9) + ((sign + 1) << 10)
            plan_ref[index * PLAN + 1 + counts[index]] = entry
            counts[index] = counts[index] + jnp.where(live & (unit >= low) & (unit < high), 1, 0)
    for index in range(KERNELS):
        plan_ref[index * PLAN] = counts[index]


def pick_kernel(meta_ref, own_ref, back_ref, far_ref, ahead_ref, out_ref):
    alpha = meta_ref[ALPHA]
    core = meta_ref[BETA] & 1
    for k in range(A_SLOTS):
        source = meta_ref[A_SOURCE + k]
        sign = meta_ref[A_SIGN + k].astype(jnp.float32).astype(out_ref.dtype)
        dz = ((source >> 2) - (alpha >> 2)) & 3
        dx = (source - alpha) & 3
        dx = jnp.where(core != 0, (4 - dx) & 3, dx)

        def put(i, k=k, sign=sign, dz=dz):
            for half in range(2):
                block = (own_ref, back_ref, far_ref, ahead_ref)[i][dz, :, half * BLK : (half + 1) * BLK]
                out_ref[half, :, k * BLK : (k + 1) * BLK] = block.T * sign

        choose(dx, 0, X_SIZE, put)


def contract_kernel(index, last, plan_ref, a_ref, b_own, b_other, *rest):
    count_units = FIRST_UNITS[index + 1] - FIRST_UNITS[index]
    units, rest = rest[:count_units], rest[count_units:]
    if index:
        sum_ref, rest = rest[0], rest[1:]
    if last:
        chol_ref, mine_ref, other_ref, acc, c_buf, b_buf, c_sem, b_sem = rest
    else:
        acc, c_buf, b_buf, c_sem, b_sem = rest
    vectors = b_own.shape[0]
    count = plan_ref[index * PLAN]
    wide_steps = count >> 2
    narrow_steps = (count - WIDE * wide_steps + 1) >> 1
    steps = wide_steps + narrow_steps

    def first_of(step):
        return jnp.where(step < wide_steps, WIDE * step, NARROW * step + (WIDE - NARROW) * wide_steps)

    def entry_of(at):
        return plan_ref[index * PLAN + 1 + jnp.minimum(at, count - 1)]

    def c_copy(unit, half, slot, lane):
        return pltpu.make_async_copy(
            unit.at[half], c_buf.at[slot, pl.ds(lane * BLK, BLK)], c_sem.at[slot, lane]
        )

    def b_copy(ref, u, l, slot, lane, part):
        vectors_of = (pl.ds(0, VECTORS_PER_GROUP), pl.ds(VECTORS_PER_GROUP, vectors - VECTORS_PER_GROUP))[part]
        return pltpu.make_async_copy(
            ref.at[vectors_of, u, l], b_buf.at[slot, lane, vectors_of], b_sem.at[slot, lane, part]
        )

    def start_c(step, slot, lanes):
        for lane in lanes:
            entry = entry_of(first_of(step) + lane)
            half = (entry >> 9) & 1
            choose((entry >> 6) & 7, 0, count_units, lambda i: c_copy(units[i], half, slot, lane).start())

    def start_b(step, slot, lanes, part):
        for lane in lanes:
            entry = entry_of(first_of(step) + lane)
            pair = entry & 63
            foreign = pair >= PAIRS
            pair = jnp.where(foreign, pair - PAIRS, pair)
            u = pair // B_SLOTS
            l = pair - u * B_SLOTS

            @pl.when(foreign)
            def _(u=u, l=l, lane=lane):
                b_copy(b_other, u, l, slot, lane, part).start()

            @pl.when(jnp.logical_not(foreign))
            def _(u=u, l=l, lane=lane):
                b_copy(b_own, u, l, slot, lane, part).start()

    def start_step(step, slot):
        def start(lanes):
            start_c(step, slot, lanes)
            for part in range(2):
                start_b(step, slot, lanes, part)

        @pl.when(step < wide_steps)
        def _():
            start(range(WIDE))

        @pl.when((step >= wide_steps) & (step < steps))
        def _():
            start(range(NARROW))

    start_step(0, 0)
    acc[...] = sum_ref[...] if index else jnp.zeros_like(acc)

    def body(width, step, carry):
        slot = step & 1
        start_step(step + 1, 1 - slot)
        for lane in range(width):
            c_copy(units[0], 0, slot, lane).wait()
        sums = [jnp.zeros((BLK, BLK), jnp.float32) for _ in range(width)]

        def panel_of(group):
            columns = slice(group * BLK, (group + VECTORS_PER_GROUP) * BLK)
            return jnp.dot(
                c_buf[slot, : width * BLK], a_ref[:, columns], preferred_element_type=jnp.float32
            ).astype(jnp.bfloat16)

        panel = panel_of(0)
        for group in range(0, vectors, VECTORS_PER_GROUP):
            following = panel_of(group + VECTORS_PER_GROUP) if group + VECTORS_PER_GROUP < vectors else None
            if group <= VECTORS_PER_GROUP:
                for lane in range(width):
                    b_copy(b_own, 0, 0, slot, lane, group // VECTORS_PER_GROUP).wait()
            for lane in range(width):
                tiles = [b_buf[slot, lane, group + r] for r in range(VECTORS_PER_GROUP)]
                blocks = [
                    panel[lane * BLK : (lane + 1) * BLK, r * BLK : (r + 1) * BLK]
                    for r in range(VECTORS_PER_GROUP)
                ]
                sums[lane] += jnp.dot(
                    jnp.concatenate(tiles, axis=1),
                    jnp.concatenate(blocks, axis=0),
                    preferred_element_type=jnp.float32,
                )
            panel = following
        for lane in range(width):
            at = first_of(step) + lane
            entry = entry_of(at)
            factor = jnp.where(at < count, (entry >> 10) - 1, 0).astype(jnp.float32)
            acc[(entry & 63) // B_SLOTS] += factor * sums[lane]
        return carry

    lax.fori_loop(0, wide_steps, functools.partial(body, WIDE), 0)
    lax.fori_loop(wide_steps, steps, functools.partial(body, NARROW), 0)
    if last:
        for shift in range(4):
            for half in range(2):
                u = ((chol_ref[0] + shift) & 3) * 2 + half
                lanes = slice(half * BLK, (half + 1) * BLK)
                mine_ref[shift, :, lanes] = acc[u].T
                other_ref[shift, :, lanes] = acc[B_BLOCKS + u].T


def contract(index, plan, a_flipped, b_own, b_other, units, running=None, chol=None):
    vectors, blocks = b_own.shape[:2]
    last = chol is not None
    part = len(units) / 8
    flops = int(part * 2 * (a_flipped.size * blocks * B_SLOTS * BLK + b_own.size * BLK))
    moved = int(part * 2 * b_own.size) + 2 * a_flipped.size
    whole = jax.ShapeDtypeStruct((2 * blocks, BLK, BLK), jnp.float32)
    shares = jax.ShapeDtypeStruct((4, BLK, blocks * BLK // 4), jnp.float32)
    sums = [] if running is None else [running]
    chols = [chol] if last else []
    return pl.pallas_call(
        functools.partial(contract_kernel, index, last),
        out_shape=[shares, shares] if last else whole,
        in_specs=[SMEM, VMEM, HBM, HBM] + [HBM] * len(units) + [VMEM] * len(sums) + [SMEM] * len(chols),
        out_specs=[VMEM, VMEM] if last else VMEM,
        scratch_shapes=[pltpu.VMEM(whole.shape, jnp.float32)] * last
        + [
            pltpu.VMEM((2, WIDE * BLK, A_SLOTS * BLK), jnp.bfloat16),
            pltpu.VMEM((2, WIDE, vectors, BLK, BLK), jnp.bfloat16),
            pltpu.SemaphoreType.DMA((2, WIDE)),
            pltpu.SemaphoreType.DMA((2, WIDE, 2)),
        ],
        compiler_params=pltpu.CompilerParams(vmem_limit_bytes=47 * 1024 * 1024),
        cost_estimate=pl.CostEstimate(flops=flops, bytes_accessed=moved, transcendentals=0),
    )(plan, a_flipped, b_own, b_other, *units, *sums, *chols)


def merge_kernel(mine_ref, arrived_ref, own_ref, *piece_refs):
    own_ref[...] = mine_ref[0] + arrived_ref[0]
    for shift, piece_ref in enumerate(piece_refs, 1):
        piece_ref[...] = (mine_ref[shift] + arrived_ref[shift]).astype(piece_ref.dtype)


def merge(mine, arrived):
    shape = mine.shape[1:]
    return pl.pallas_call(
        merge_kernel,
        out_shape=[jax.ShapeDtypeStruct(shape, jnp.float32)] + [jax.ShapeDtypeStruct(shape, jnp.bfloat16)] * 3,
        in_specs=[VMEM, VMEM],
        out_specs=[VMEM] * 4,
        compiler_params=pltpu.CompilerParams(vmem_limit_bytes=8 * 1024 * 1024),
    )(mine, arrived)


def flip(a_tiles):
    vectors = a_tiles.shape[0]
    return pl.pallas_call(
        flip_kernel,
        out_shape=jax.ShapeDtypeStruct((A_SLOTS * BLK, vectors * BLK), a_tiles.dtype),
        in_specs=[HBM],
        out_specs=VMEM,
        scratch_shapes=[pltpu.VMEM(a_tiles.shape, a_tiles.dtype), pltpu.SemaphoreType.DMA((4,))],
        compiler_params=pltpu.CompilerParams(vmem_limit_bytes=48 * 1024 * 1024),
        cost_estimate=pl.CostEstimate(flops=0, bytes_accessed=4 * a_tiles.size, transcendentals=0),
    )(a_tiles)


def make_plan(meta):
    return pl.pallas_call(
        plan_kernel,
        out_shape=jax.ShapeDtypeStruct((KERNELS * PLAN,), jnp.int32),
        in_specs=[SMEM],
        out_specs=SMEM,
    )(meta)


def gather_sources(meta, quarter, b_tiles, sizes):
    alphas, betas = sizes["alpha"], sizes["beta"]
    zs = alphas // X_SIZE

    def z_from(value, distance):
        return shifted(value, "alpha", alphas, lambda i: (i // X_SIZE - distance) % zs * X_SIZE + i % X_SIZE)

    def by_core(value, sense):
        def moved(i):
            alpha, beta = i // betas, i % betas
            x = (alpha + (sense if beta % 2 == 0 else -sense)) % X_SIZE
            return (alpha // X_SIZE * X_SIZE + x) * betas + beta

        return shifted(value, ("alpha", "beta"), alphas * betas, moved)

    others = [z_from(quarter, distance) for distance in (1, 2, 3)]
    others, meta, b_held = lax.optimization_barrier((others, meta, b_tiles))
    own = jnp.stack([quarter] + others)
    ahead, back = by_core(own, 1), by_core(own, -1)
    ahead, plan = lax.optimization_barrier((ahead, make_plan(meta)))
    far = by_core(ahead, 1)
    unit = pl.pallas_call(
        pick_kernel,
        out_shape=jax.ShapeDtypeStruct((2, BLK, A_SLOTS * BLK), quarter.dtype),
        in_specs=[SMEM] + [VMEM] * 4,
        out_specs=VMEM,
        compiler_params=pltpu.CompilerParams(vmem_limit_bytes=8 * 1024 * 1024),
    )(meta, own, back, far, ahead)
    return plan, unit, b_held


def gather_and_contract(plan, chol, unit, a_tiles, b_own, b_other, sizes):
    betas, chols = sizes["beta"], sizes["chol"]

    def z_other(value):
        return shifted(value, "beta", betas, lambda i: i ^ 2)

    def by_core(value, sense):
        def moved(i):
            beta, chol = i // chols, i % chols
            return beta * chols + (chol + (sense if beta % 2 == 0 else -sense)) % chols

        return shifted(value, ("beta", "chol"), betas * chols, moved)

    ahead, across, back = by_core(unit, 1), z_other(unit), by_core(unit, -1)
    tiles = (plan, flip(a_tiles), b_own, b_other)
    running = contract(0, *tiles, [unit])
    running, ahead, across, back = lax.optimization_barrier((running, ahead, across, back))
    middle, far_ahead, far_back = by_core(ahead, 1), z_other(ahead), by_core(across, -1)
    running = contract(1, *tiles, [ahead, across, back], running)
    running, middle, far_back, far_ahead = lax.optimization_barrier((running, middle, far_back, far_ahead))
    far_middle = by_core(far_ahead, 1)
    running = contract(2, *tiles, [middle, far_back, far_ahead], running)
    running, far_middle = lax.optimization_barrier((running, far_middle))
    return contract(3, *tiles, [far_middle], running, chol=chol)


def per_device(sizes, ci_vector, a_tiles, a_source, a_sign, b_tiles, b_source, b_sign):
    betas, chols = sizes["beta"], sizes["chol"]

    def core_other(value):
        return shifted(value, "beta", betas, lambda i: i ^ 1)

    chol = lax.axis_index("chol").astype(jnp.int32)
    width = ci_vector.shape[1] // chols
    quarter = lax.dynamic_slice_in_dim(ci_vector, chol * width, width, axis=1)
    place = jnp.stack([lax.axis_index("alpha"), lax.axis_index("beta"), chol]).astype(jnp.int32)
    pairs = jnp.concatenate([b_source.reshape(-1), b_sign.reshape(-1)])
    meta = jnp.concatenate([place, a_source.reshape(-1), a_sign.reshape(-1), pairs, core_other(pairs)])
    plan, unit, b_held = gather_sources(meta, quarter, b_tiles, sizes)
    b_other = core_other(b_held)
    mine, other = gather_and_contract(plan, chol[None], unit, a_tiles, b_tiles, b_other, sizes)
    own, *pieces = merge(mine, core_other(other))
    for shift, piece in enumerate(pieces, 1):
        own = own + shifted(piece, "chol", chols, lambda i: (i + shift) % chols).astype(jnp.float32)
    return own.astype(jnp.bfloat16)


def solution(mesh):
    placed = (
        P("alpha", "beta"),
        P("chol", "alpha", None, None, None),
        P("alpha", None),
        P("alpha", None),
        P("chol", "beta", None, None, None),
        P("beta", None),
        P("beta", None),
    )
    sizes = dict(mesh.shape)

    def body(*args):
        return per_device(sizes, *args)

    return jax.shard_map(
        body,
        mesh=mesh,
        in_specs=placed,
        out_specs=P("alpha", ("beta", "chol")),
        check_vma=False,
    )
```

```python
import functools

import jax
import jax.numpy as jnp
from jax import lax
from jax.experimental import pallas as pl
from jax.experimental.pallas import tpu as pltpu
from jax.sharding import PartitionSpec as P

BLK = 128
VECTORS_PER_GROUP = 8
WIDE, NARROW = 4, 2
X_SIZE = 4
A_SLOTS, B_SLOTS, B_BLOCKS = 6, 3, 8
PAIRS = B_SLOTS * B_BLOCKS
ALPHA, BETA, CHOL, A_SOURCE = 0, 1, 2, 3
A_SIGN = A_SOURCE + A_SLOTS
B_SOURCE = A_SIGN + A_SLOTS
B_SIGN = B_SOURCE + PAIRS
OTHER = 2 * PAIRS
ARRIVAL = 0x67521430
UNITS = (range(0, 1), range(1, 4), range(4, 7), range(7, 8), range(6, 8))
OWN_UNITS = (UNITS[0], UNITS[1], range(4, 6), range(0), UNITS[4])
OTHER_UNITS = (UNITS[0], UNITS[1], UNITS[2], UNITS[3], range(0))
KERNELS, FOR_OTHER = len(UNITS), 3
PLAN = 64
SMEM = pl.BlockSpec(memory_space=pltpu.SMEM)
VMEM = pl.BlockSpec(memory_space=pltpu.VMEM)
HBM = pl.BlockSpec(memory_space=pltpu.HBM)


def shifted(value, axis, size, moves_to):
    return lax.ppermute(value, axis, [(i, moves_to(i)) for i in range(size)])


def choose(index, low, high, act):
    if high - low == 1:
        act(low)
        return
    middle = (low + high) // 2

    @pl.when(index < middle)
    def _():
        choose(index, low, middle, act)

    @pl.when(index >= middle)
    def _():
        choose(index, middle, high, act)


def flip_kernel(a_hbm, out_ref, a_buf, sems):
    parts = sems.shape[0]
    size = a_buf.shape[0] // parts
    copies = [
        pltpu.make_async_copy(a_hbm.at[pl.ds(p * size, size)], a_buf.at[pl.ds(p * size, size)], sems.at[p])
        for p in range(parts)
    ]
    for copy in copies:
        copy.start()
    for p, copy in enumerate(copies):
        copy.wait()
        for q in range(p * size, (p + 1) * size):
            for k in range(A_SLOTS):
                out_ref[k * BLK : (k + 1) * BLK, q * BLK : (q + 1) * BLK] = a_buf[q, 0, k].T


def plan_kernel(meta_ref, plan_ref):
    beta, chol = meta_ref[BETA], meta_ref[CHOL]
    core = beta & 1
    counts = [jnp.int32(0)] * KERNELS
    for pair in range(2 * PAIRS):
        base = OTHER if pair >= PAIRS else 0
        m = meta_ref[B_SOURCE + base + pair % PAIRS]
        sign = meta_ref[B_SIGN + base + pair % PAIRS]
        owner = m >> 3
        dy = ((m >> 1) - chol) & 3
        dy = jnp.where(core != 0, (4 - dy) & 3, dy)
        unit = (jnp.int32(ARRIVAL) >> (4 * (((owner ^ beta) & 2) * 2 + dy))) & 7
        live = (sign != 0) & ((owner & 1) == core)
        for index in range(KERNELS):
            used = (OTHER_UNITS if pair >= PAIRS else OWN_UNITS)[index]
            if not used:
                continue
            entry = pair + ((unit - UNITS[index].start) << 6) + ((m & 1) << 9) + ((sign + 1) << 10)
            plan_ref[index * PLAN + 1 + counts[index]] = entry
            here = live & (unit >= used.start) & (unit < used.stop)
            counts[index] = counts[index] + jnp.where(here, 1, 0)
    for index in range(KERNELS):
        plan_ref[index * PLAN] = counts[index]


def pick_kernel(meta_ref, own_ref, back_ref, far_ref, ahead_ref, out_ref):
    alpha = meta_ref[ALPHA]
    core = meta_ref[BETA] & 1
    for k in range(A_SLOTS):
        source = meta_ref[A_SOURCE + k]
        sign = meta_ref[A_SIGN + k].astype(jnp.float32).astype(out_ref.dtype)
        dz = ((source >> 2) - (alpha >> 2)) & 3
        dx = (source - alpha) & 3
        dx = jnp.where(core != 0, (4 - dx) & 3, dx)

        def put(i, k=k, sign=sign, dz=dz):
            for half in range(2):
                block = (own_ref, back_ref, far_ref, ahead_ref)[i][dz, :, half * BLK : (half + 1) * BLK]
                out_ref[half, :, k * BLK : (k + 1) * BLK] = block.T * sign

        choose(dx, 0, X_SIZE, put)


def contract_kernel(index, plan_ref, a_ref, b_own, b_other, *rest):
    count_units = len(UNITS[index])
    units, rest = rest[:count_units], rest[count_units:]
    if index:
        sum_ref, rest = rest[0], rest[1:]
    last = index >= FOR_OTHER
    if last:
        chol_ref, share_ref, acc, c_buf, b_buf, b_sem = rest
    else:
        acc, c_buf, b_buf, b_sem = rest
    first_block = B_BLOCKS if index == FOR_OTHER else 0
    vectors = b_own.shape[0]
    count = plan_ref[index * PLAN]
    wide_steps = count >> 2
    narrow_steps = (count - WIDE * wide_steps + 1) >> 1
    steps = wide_steps + narrow_steps

    def first_of(step):
        return jnp.where(step < wide_steps, WIDE * step, NARROW * step + (WIDE - NARROW) * wide_steps)

    def entry_of(at):
        return plan_ref[index * PLAN + 1 + jnp.minimum(at, count - 1)]

    def b_copy(ref, u, l, slot, lane, part):
        vectors_of = (pl.ds(0, VECTORS_PER_GROUP), pl.ds(VECTORS_PER_GROUP, vectors - VECTORS_PER_GROUP))[part]
        return pltpu.make_async_copy(
            ref.at[vectors_of, u, l], b_buf.at[slot, lane, vectors_of], b_sem.at[slot, lane, part]
        )

    def start_b(step, slot, lanes, part):
        for lane in lanes:
            entry = entry_of(first_of(step) + lane)
            pair = entry & 63
            foreign = pair >= PAIRS
            pair = jnp.where(foreign, pair - PAIRS, pair)
            u = pair // B_SLOTS
            l = pair - u * B_SLOTS

            @pl.when(foreign)
            def _(u=u, l=l, lane=lane):
                b_copy(b_other, u, l, slot, lane, part).start()

            @pl.when(jnp.logical_not(foreign))
            def _(u=u, l=l, lane=lane):
                b_copy(b_own, u, l, slot, lane, part).start()

    def start_step(step, slot):
        def start(lanes):
            for part in range(2):
                start_b(step, slot, lanes, part)

        @pl.when(step < wide_steps)
        def _():
            start(range(WIDE))

        @pl.when((step >= wide_steps) & (step < steps))
        def _():
            start(range(NARROW))

    start_step(0, 0)
    acc[...] = sum_ref[first_block : first_block + acc.shape[0]] if index else jnp.zeros_like(acc)

    def body(width, step, carry):
        slot = step & 1
        start_step(step + 1, 1 - slot)
        for lane in range(width):
            entry = entry_of(first_of(step) + lane)
            half = (entry >> 9) & 1

            def fill(i, lane=lane, half=half):
                c_buf[lane * BLK : (lane + 1) * BLK] = units[i][half]

            choose((entry >> 6) & 7, 0, count_units, fill)
        sums = [jnp.zeros((BLK, BLK), jnp.float32) for _ in range(width)]

        def panel_of(group):
            columns = slice(group * BLK, (group + VECTORS_PER_GROUP) * BLK)
            return jnp.dot(
                c_buf[: width * BLK], a_ref[:, columns], preferred_element_type=jnp.float32
            ).astype(jnp.bfloat16)

        panel = panel_of(0)
        for group in range(0, vectors, VECTORS_PER_GROUP):
            following = panel_of(group + VECTORS_PER_GROUP) if group + VECTORS_PER_GROUP < vectors else None
            if group <= VECTORS_PER_GROUP:
                for lane in range(width):
                    b_copy(b_own, 0, 0, slot, lane, group // VECTORS_PER_GROUP).wait()
            for lane in range(width):
                tiles = [b_buf[slot, lane, group + r] for r in range(VECTORS_PER_GROUP)]
                blocks = [
                    panel[lane * BLK : (lane + 1) * BLK, r * BLK : (r + 1) * BLK]
                    for r in range(VECTORS_PER_GROUP)
                ]
                sums[lane] += jnp.dot(
                    jnp.concatenate(tiles, axis=1),
                    jnp.concatenate(blocks, axis=0),
                    preferred_element_type=jnp.float32,
                )
            panel = following
        for lane in range(width):
            at = first_of(step) + lane
            entry = entry_of(at)
            factor = jnp.where(at < count, (entry >> 10) - 1, 0).astype(jnp.float32)
            acc[(entry & 63) // B_SLOTS - first_block] += factor * sums[lane]
        return carry

    lax.fori_loop(0, wide_steps, functools.partial(body, WIDE), 0)
    lax.fori_loop(wide_steps, steps, functools.partial(body, NARROW), 0)
    if last:
        for shift in range(4):
            for half in range(2):
                u = ((chol_ref[0] + shift) & 3) * 2 + half
                share_ref[shift, :, half * BLK : (half + 1) * BLK] = acc[u].T


def contract(index, plan, a_flipped, b_own, b_other, units, running=None, chol=None):
    vectors, blocks = b_own.shape[:2]
    last = index >= FOR_OTHER
    part = (len(OWN_UNITS[index]) + len(OTHER_UNITS[index])) / 16
    flops = int(part * 2 * (a_flipped.size * blocks * B_SLOTS * BLK + b_own.size * BLK))
    moved = int(part * 2 * b_own.size) + 2 * a_flipped.size
    whole = jax.ShapeDtypeStruct((2 * blocks, BLK, BLK), jnp.float32)
    shares = jax.ShapeDtypeStruct((4, BLK, blocks * BLK // 4), jnp.float32)
    sums = [] if running is None else [running]
    chols = [chol] if last else []
    return pl.pallas_call(
        functools.partial(contract_kernel, index),
        out_shape=shares if last else whole,
        in_specs=[SMEM, VMEM, HBM, HBM] + [VMEM] * (len(units) + len(sums)) + [SMEM] * len(chols),
        out_specs=VMEM,
        scratch_shapes=[pltpu.VMEM((blocks, BLK, BLK), jnp.float32)] * last
        + [
            pltpu.VMEM((WIDE * BLK, A_SLOTS * BLK), jnp.bfloat16),
            pltpu.VMEM((2, WIDE, vectors, BLK, BLK), jnp.bfloat16),
            pltpu.SemaphoreType.DMA((2, WIDE, 2)),
        ],
        compiler_params=pltpu.CompilerParams(vmem_limit_bytes=47 * 1024 * 1024),
        cost_estimate=pl.CostEstimate(flops=flops, bytes_accessed=moved, transcendentals=0),
    )(plan, a_flipped, b_own, b_other, *units, *sums, *chols)


def merge_kernel(mine_ref, arrived_ref, own_ref, *piece_refs):
    own_ref[...] = mine_ref[0] + arrived_ref[0]
    for shift, piece_ref in enumerate(piece_refs, 1):
        piece_ref[...] = (mine_ref[shift] + arrived_ref[shift]).astype(piece_ref.dtype)


def merge(mine, arrived):
    shape = mine.shape[1:]
    return pl.pallas_call(
        merge_kernel,
        out_shape=[jax.ShapeDtypeStruct(shape, jnp.float32)] + [jax.ShapeDtypeStruct(shape, jnp.bfloat16)] * 3,
        in_specs=[VMEM, VMEM],
        out_specs=[VMEM] * 4,
        compiler_params=pltpu.CompilerParams(vmem_limit_bytes=8 * 1024 * 1024),
    )(mine, arrived)


def flip(a_tiles):
    vectors = a_tiles.shape[0]
    return pl.pallas_call(
        flip_kernel,
        out_shape=jax.ShapeDtypeStruct((A_SLOTS * BLK, vectors * BLK), a_tiles.dtype),
        in_specs=[HBM],
        out_specs=VMEM,
        scratch_shapes=[pltpu.VMEM(a_tiles.shape, a_tiles.dtype), pltpu.SemaphoreType.DMA((4,))],
        compiler_params=pltpu.CompilerParams(vmem_limit_bytes=48 * 1024 * 1024),
        cost_estimate=pl.CostEstimate(flops=0, bytes_accessed=4 * a_tiles.size, transcendentals=0),
    )(a_tiles)


def make_plan(meta):
    return pl.pallas_call(
        plan_kernel,
        out_shape=jax.ShapeDtypeStruct((KERNELS * PLAN,), jnp.int32),
        in_specs=[SMEM],
        out_specs=SMEM,
    )(meta)


def gather_sources(meta, quarter, b_tiles, sizes):
    alphas, betas = sizes["alpha"], sizes["beta"]
    zs = alphas // X_SIZE

    def z_from(value, distance):
        return shifted(value, "alpha", alphas, lambda i: (i // X_SIZE - distance) % zs * X_SIZE + i % X_SIZE)

    def by_core(value, sense):
        def moved(i):
            alpha, beta = i // betas, i % betas
            x = (alpha + (sense if beta % 2 == 0 else -sense)) % X_SIZE
            return (alpha // X_SIZE * X_SIZE + x) * betas + beta

        return shifted(value, ("alpha", "beta"), alphas * betas, moved)

    others = [z_from(quarter, distance) for distance in (1, 2, 3)]
    others, meta, b_held = lax.optimization_barrier((others, meta, b_tiles))
    own = jnp.stack([quarter] + others)
    ahead, back = by_core(own, 1), by_core(own, -1)
    ahead, plan = lax.optimization_barrier((ahead, make_plan(meta)))
    far = by_core(ahead, 1)
    unit = pl.pallas_call(
        pick_kernel,
        out_shape=jax.ShapeDtypeStruct((2, BLK, A_SLOTS * BLK), quarter.dtype),
        in_specs=[SMEM] + [VMEM] * 4,
        out_specs=VMEM,
        compiler_params=pltpu.CompilerParams(vmem_limit_bytes=8 * 1024 * 1024),
    )(meta, own, back, far, ahead)
    return plan, unit, b_held


def gather_and_contract(plan, chol, unit, a_tiles, b_own, b_other, sizes):
    betas, chols = sizes["beta"], sizes["chol"]

    def z_other(value):
        return shifted(value, "beta", betas, lambda i: i ^ 2)

    def by_core(value, sense):
        def moved(i):
            beta, chol = i // chols, i % chols
            return beta * chols + (chol + (sense if beta % 2 == 0 else -sense)) % chols

        return shifted(value, ("beta", "chol"), betas * chols, moved)

    ahead, across, back = by_core(unit, 1), z_other(unit), by_core(unit, -1)
    tiles = (plan, flip(a_tiles), b_own, b_other)
    running = contract(0, *tiles, [unit])
    running, ahead, across, back = lax.optimization_barrier((running, ahead, across, back))
    middle, far_ahead, far_back = by_core(ahead, 1), z_other(ahead), by_core(across, -1)
    running = contract(1, *tiles, [ahead, across, back], running)
    running, middle, far_back, far_ahead = lax.optimization_barrier((running, middle, far_back, far_ahead))
    far_middle = by_core(far_ahead, 1)
    running = contract(2, *tiles, [middle, far_back, far_ahead], running)
    running, far_middle = lax.optimization_barrier((running, far_middle))
    other = contract(FOR_OTHER, *tiles, [far_middle], running, chol)
    return contract(4, *tiles, [far_ahead, far_middle], running, chol), other


def per_device(sizes, ci_vector, a_tiles, a_source, a_sign, b_tiles, b_source, b_sign):
    betas, chols = sizes["beta"], sizes["chol"]

    def core_other(value):
        return shifted(value, "beta", betas, lambda i: i ^ 1)

    chol = lax.axis_index("chol").astype(jnp.int32)
    width = ci_vector.shape[1] // chols
    quarter = lax.dynamic_slice_in_dim(ci_vector, chol * width, width, axis=1)
    place = jnp.stack([lax.axis_index("alpha"), lax.axis_index("beta"), chol]).astype(jnp.int32)
    pairs = jnp.concatenate([b_source.reshape(-1), b_sign.reshape(-1)])
    meta = jnp.concatenate([place, a_source.reshape(-1), a_sign.reshape(-1), pairs, core_other(pairs)])
    plan, unit, b_held = gather_sources(meta, quarter, b_tiles, sizes)
    b_other = core_other(b_held)
    mine, other = gather_and_contract(plan, chol[None], unit, a_tiles, b_tiles, b_other, sizes)
    own, *pieces = merge(mine, core_other(other))
    for shift, piece in enumerate(pieces, 1):
        own = own + shifted(piece, "chol", chols, lambda i: (i + shift) % chols).astype(jnp.float32)
    return own.astype(jnp.bfloat16)


def solution(mesh):
    placed = (
        P("alpha", "beta"),
        P("chol", "alpha", None, None, None),
        P("alpha", None),
        P("alpha", None),
        P("chol", "beta", None, None, None),
        P("beta", None),
        P("beta", None),
    )
    sizes = dict(mesh.shape)

    def body(*args):
        return per_device(sizes, *args)

    return jax.shard_map(
        body,
        mesh=mesh,
        in_specs=placed,
        out_specs=P("alpha", ("beta", "chol")),
        check_vma=False,
    )
```

```python
import functools

import jax
import jax.numpy as jnp
from jax import lax
from jax.experimental import pallas as pl
from jax.experimental.pallas import tpu as pltpu
from jax.sharding import PartitionSpec as P

BLK = 128
VECTORS_PER_GROUP = 8
WIDE, NARROW = 4, 2
X_SIZE = 4
A_SLOTS, B_SLOTS, B_BLOCKS = 6, 3, 8
PAIRS = B_SLOTS * B_BLOCKS
ALPHA, BETA, CHOL, A_SOURCE = 0, 1, 2, 3
A_SIGN = A_SOURCE + A_SLOTS
B_SOURCE = A_SIGN + A_SLOTS
B_SIGN = B_SOURCE + PAIRS
OTHER = 2 * PAIRS
ARRIVAL = 0x67521430
FIRST_UNITS = (0, 1, 4, 7, 8)
KERNELS = len(FIRST_UNITS) - 1
LAST = KERNELS - 1
PLAN = 64
SMEM = pl.BlockSpec(memory_space=pltpu.SMEM)
VMEM = pl.BlockSpec(memory_space=pltpu.VMEM)
HBM = pl.BlockSpec(memory_space=pltpu.HBM)


def shifted(value, axis, size, moves_to):
    return lax.ppermute(value, axis, [(i, moves_to(i)) for i in range(size)])


def choose(index, low, high, act):
    if high - low == 1:
        act(low)
        return
    middle = (low + high) // 2

    @pl.when(index < middle)
    def _():
        choose(index, low, middle, act)

    @pl.when(index >= middle)
    def _():
        choose(index, middle, high, act)


def flip_kernel(a_hbm, out_ref, a_buf, sems):
    parts = sems.shape[0]
    size = a_buf.shape[0] // parts
    copies = [
        pltpu.make_async_copy(a_hbm.at[pl.ds(p * size, size)], a_buf.at[pl.ds(p * size, size)], sems.at[p])
        for p in range(parts)
    ]
    for copy in copies:
        copy.start()
    for p, copy in enumerate(copies):
        copy.wait()
        for q in range(p * size, (p + 1) * size):
            for k in range(A_SLOTS):
                out_ref[k * BLK : (k + 1) * BLK, q * BLK : (q + 1) * BLK] = a_buf[q, 0, k].T


def plan_kernel(meta_ref, plan_ref):
    beta, chol = meta_ref[BETA], meta_ref[CHOL]
    core = beta & 1
    counts = [jnp.int32(0)] * KERNELS
    for pair in range(2 * PAIRS):
        base = OTHER if pair >= PAIRS else 0
        m = meta_ref[B_SOURCE + base + pair % PAIRS]
        sign = meta_ref[B_SIGN + base + pair % PAIRS]
        owner = m >> 3
        dy = ((m >> 1) - chol) & 3
        dy = jnp.where(core != 0, (4 - dy) & 3, dy)
        unit = (jnp.int32(ARRIVAL) >> (4 * (((owner ^ beta) & 2) * 2 + dy))) & 7
        live = (sign != 0) & ((owner & 1) == core)
        for index in range(KERNELS):
            low, high = FIRST_UNITS[index], FIRST_UNITS[index + 1]
            where = (m & 1) << 6 if index == LAST else ((unit - low) << 6) + ((m & 1) << 9)
            plan_ref[index * PLAN + 1 + counts[index]] = pair + where + ((sign + 1) << 10)
            counts[index] = counts[index] + jnp.where(live & (unit >= low) & (unit < high), 1, 0)
    for index in range(KERNELS):
        plan_ref[index * PLAN] = counts[index]


def pick_kernel(meta_ref, *refs):
    stacks, out_ref = refs[:-1], refs[-1]
    alpha = meta_ref[ALPHA]
    core = meta_ref[BETA] & 1
    for k in range(A_SLOTS):
        source = meta_ref[A_SOURCE + k]
        sign = meta_ref[A_SIGN + k].astype(jnp.float32).astype(out_ref.dtype)
        dz = ((source >> 2) - (alpha >> 2)) & 3
        dx = (source - alpha) & 3
        dx = jnp.where(core != 0, (4 - dx) & 3, dx)
        which = jnp.where(dx == 2, 2 + (dz >> 1), dx + (dx >> 1 & dx))
        place = jnp.where(dx == 2, dz & 1, dz)

        def put(i, k=k, sign=sign, place=place):
            for half in range(2):
                block = stacks[i][place, :, half * BLK : (half + 1) * BLK]
                out_ref[half, :, k * BLK : (k + 1) * BLK] = block.T * sign

        choose(which, 0, len(stacks), put)


def contract_kernel(index, plan_ref, a_ref, b_own, b_other, *rest):
    count_units = 2 if index == LAST else FIRST_UNITS[index + 1] - FIRST_UNITS[index]
    units, rest = rest[:count_units], rest[count_units:]
    if index:
        sum_ref, rest = rest[0], rest[1:]
    if index == LAST:
        chol_ref, mine_ref, other_ref, acc, c_buf, b_buf, b_sem = rest
    else:
        acc, c_buf, b_buf, b_sem = rest
    vectors = b_own.shape[0]
    count = plan_ref[index * PLAN]
    wide_steps = count >> 2
    narrow_steps = (count - WIDE * wide_steps + 1) >> 1
    steps = wide_steps + narrow_steps

    def first_of(step):
        return jnp.where(step < wide_steps, WIDE * step, NARROW * step + (WIDE - NARROW) * wide_steps)

    def entry_of(at):
        return plan_ref[index * PLAN + 1 + jnp.minimum(at, count - 1)]

    def b_copy(ref, u, l, slot, lane, part):
        vectors_of = (pl.ds(0, VECTORS_PER_GROUP), pl.ds(VECTORS_PER_GROUP, vectors - VECTORS_PER_GROUP))[part]
        return pltpu.make_async_copy(
            ref.at[vectors_of, u, l], b_buf.at[slot, lane, vectors_of], b_sem.at[slot, lane, part]
        )

    def start_b(step, slot, lanes, part):
        for lane in lanes:
            entry = entry_of(first_of(step) + lane)
            pair = entry & 63
            foreign = pair >= PAIRS
            pair = jnp.where(foreign, pair - PAIRS, pair)
            u = pair // B_SLOTS
            l = pair - u * B_SLOTS

            @pl.when(foreign)
            def _(u=u, l=l, lane=lane):
                b_copy(b_other, u, l, slot, lane, part).start()

            @pl.when(jnp.logical_not(foreign))
            def _(u=u, l=l, lane=lane):
                b_copy(b_own, u, l, slot, lane, part).start()

    def start_step(step, slot):
        def start(lanes):
            for part in range(2):
                start_b(step, slot, lanes, part)

        @pl.when(step < wide_steps)
        def _():
            start(range(WIDE))

        @pl.when((step >= wide_steps) & (step < steps))
        def _():
            start(range(NARROW))

    start_step(0, 0)
    acc[...] = sum_ref[...] if index else jnp.zeros_like(acc)

    def body(width, step, carry):
        slot = step & 1
        start_step(step + 1, 1 - slot)
        for lane in range(width):
            entry = entry_of(first_of(step) + lane)
            half = (entry >> 9) & 1

            def fill(i, lane=lane, half=half):
                c_buf[lane * BLK : (lane + 1) * BLK] = units[i][half]

            choose((entry >> 6) & 7, 0, count_units, fill)
        sums = [jnp.zeros((BLK, BLK), jnp.float32) for _ in range(width)]

        def panel_of(group):
            columns = slice(group * BLK, (group + VECTORS_PER_GROUP) * BLK)
            return jnp.dot(
                c_buf[: width * BLK], a_ref[:, columns], preferred_element_type=jnp.float32
            ).astype(jnp.bfloat16)

        panel = panel_of(0)
        for group in range(0, vectors, VECTORS_PER_GROUP):
            following = panel_of(group + VECTORS_PER_GROUP) if group + VECTORS_PER_GROUP < vectors else None
            if group <= VECTORS_PER_GROUP:
                for lane in range(width):
                    b_copy(b_own, 0, 0, slot, lane, group // VECTORS_PER_GROUP).wait()
            for lane in range(width):
                tiles = [b_buf[slot, lane, group + r] for r in range(VECTORS_PER_GROUP)]
                blocks = [
                    panel[lane * BLK : (lane + 1) * BLK, r * BLK : (r + 1) * BLK]
                    for r in range(VECTORS_PER_GROUP)
                ]
                sums[lane] += jnp.dot(
                    jnp.concatenate(tiles, axis=1),
                    jnp.concatenate(blocks, axis=0),
                    preferred_element_type=jnp.float32,
                )
            panel = following
        for lane in range(width):
            at = first_of(step) + lane
            entry = entry_of(at)
            factor = jnp.where(at < count, (entry >> 10) - 1, 0).astype(jnp.float32)
            acc[(entry & 63) // B_SLOTS] += factor * sums[lane]
        return carry

    lax.fori_loop(0, wide_steps, functools.partial(body, WIDE), 0)
    lax.fori_loop(wide_steps, steps, functools.partial(body, NARROW), 0)
    if index == LAST:
        for shift in range(4):
            for half in range(2):
                u = ((chol_ref[0] + shift) & 3) * 2 + half
                lanes = slice(half * BLK, (half + 1) * BLK)
                mine_ref[shift, :, lanes] = acc[u].T
                other_ref[shift, :, lanes] = acc[B_BLOCKS + u].T


def contract(index, plan, a_flipped, b_own, b_other, units, running=None, chol=None):
    vectors, blocks = b_own.shape[:2]
    last = index == LAST
    part = (FIRST_UNITS[index + 1] - FIRST_UNITS[index]) / 8
    flops = int(part * 2 * (a_flipped.size * blocks * B_SLOTS * BLK + b_own.size * BLK))
    moved = int(part * 2 * b_own.size) + 2 * a_flipped.size
    whole = jax.ShapeDtypeStruct((2 * blocks, BLK, BLK), jnp.float32)
    shares = jax.ShapeDtypeStruct((4, BLK, blocks * BLK // 4), jnp.float32)
    sums = [] if running is None else [running]
    chols = [chol] if last else []
    return pl.pallas_call(
        functools.partial(contract_kernel, index),
        out_shape=[shares, shares] if last else whole,
        in_specs=[SMEM, VMEM, HBM, HBM] + [VMEM] * (len(units) + len(sums)) + [SMEM] * len(chols),
        out_specs=[VMEM, VMEM] if last else VMEM,
        scratch_shapes=[pltpu.VMEM(whole.shape, jnp.float32)] * last
        + [
            pltpu.VMEM((WIDE * BLK, A_SLOTS * BLK), jnp.bfloat16),
            pltpu.VMEM((2, WIDE, vectors, BLK, BLK), jnp.bfloat16),
            pltpu.SemaphoreType.DMA((2, WIDE, 2)),
        ],
        compiler_params=pltpu.CompilerParams(vmem_limit_bytes=47 * 1024 * 1024),
        cost_estimate=pl.CostEstimate(flops=flops, bytes_accessed=moved, transcendentals=0),
    )(plan, a_flipped, b_own, b_other, *units, *sums, *chols)


def merge_kernel(mine_ref, arrived_ref, own_ref, *piece_refs):
    own_ref[...] = mine_ref[0] + arrived_ref[0]
    for shift, piece_ref in enumerate(piece_refs, 1):
        piece_ref[...] = (mine_ref[shift] + arrived_ref[shift]).astype(piece_ref.dtype)


def merge(mine, arrived):
    shape = mine.shape[1:]
    return pl.pallas_call(
        merge_kernel,
        out_shape=[jax.ShapeDtypeStruct(shape, jnp.float32)] + [jax.ShapeDtypeStruct(shape, jnp.bfloat16)] * 3,
        in_specs=[VMEM, VMEM],
        out_specs=[VMEM] * 4,
        compiler_params=pltpu.CompilerParams(vmem_limit_bytes=8 * 1024 * 1024),
    )(mine, arrived)


def flip(a_tiles):
    vectors = a_tiles.shape[0]
    return pl.pallas_call(
        flip_kernel,
        out_shape=jax.ShapeDtypeStruct((A_SLOTS * BLK, vectors * BLK), a_tiles.dtype),
        in_specs=[HBM],
        out_specs=VMEM,
        scratch_shapes=[pltpu.VMEM(a_tiles.shape, a_tiles.dtype), pltpu.SemaphoreType.DMA((4,))],
        compiler_params=pltpu.CompilerParams(vmem_limit_bytes=48 * 1024 * 1024),
        cost_estimate=pl.CostEstimate(flops=0, bytes_accessed=4 * a_tiles.size, transcendentals=0),
    )(a_tiles)


def make_plan(meta):
    return pl.pallas_call(
        plan_kernel,
        out_shape=jax.ShapeDtypeStruct((KERNELS * PLAN,), jnp.int32),
        in_specs=[SMEM],
        out_specs=SMEM,
    )(meta)


def gather_sources(meta, other_pairs, quarter, b_tiles, sizes):
    alphas, betas = sizes["alpha"], sizes["beta"]
    zs = alphas // X_SIZE

    def z_from(value, distance):
        return shifted(value, "alpha", alphas, lambda i: (i // X_SIZE - distance) % zs * X_SIZE + i % X_SIZE)

    def by_core(value, sense):
        def moved(i):
            alpha, beta = i // betas, i % betas
            x = (alpha + (sense if beta % 2 == 0 else -sense)) % X_SIZE
            return (alpha // X_SIZE * X_SIZE + x) * betas + beta

        return shifted(value, ("alpha", "beta"), alphas * betas, moved)

    others = [z_from(quarter, distance) for distance in (1, 2, 3)]
    others, other_pairs, b_held = lax.optimization_barrier((others, other_pairs, b_tiles))
    meta = jnp.concatenate([meta, other_pairs])
    own = jnp.stack([quarter] + others)
    ahead, back = by_core(own, 1), by_core(own, -1)
    ahead, plan = lax.optimization_barrier((ahead, make_plan(meta)))
    far_low, far_high = by_core(ahead[:2], 1), by_core(back[2:], -1)
    unit = pl.pallas_call(
        pick_kernel,
        out_shape=jax.ShapeDtypeStruct((2, BLK, A_SLOTS * BLK), quarter.dtype),
        in_specs=[SMEM] + [VMEM] * 5,
        out_specs=VMEM,
        compiler_params=pltpu.CompilerParams(vmem_limit_bytes=8 * 1024 * 1024),
    )(meta, own, back, far_low, far_high, ahead)
    return plan, unit, b_held


def gather_and_contract(plan, chol, unit, a_tiles, b_own, b_other, sizes):
    betas, chols = sizes["beta"], sizes["chol"]

    def z_other(value):
        return shifted(value, "beta", betas, lambda i: i ^ 2)

    def by_core(value, sense):
        def moved(i):
            beta, chol = i // chols, i % chols
            return beta * chols + (chol + (sense if beta % 2 == 0 else -sense)) % chols

        return shifted(value, ("beta", "chol"), betas * chols, moved)

    ahead, across, back = by_core(unit, 1), z_other(unit), by_core(unit, -1)
    tiles = (plan, flip(a_tiles), b_own, b_other)
    running = contract(0, *tiles, [unit])
    running, ahead, across, back = lax.optimization_barrier((running, ahead, across, back))
    middle, far_ahead, far_back = by_core(ahead, 1), z_other(ahead), by_core(across, -1)
    running = contract(1, *tiles, [ahead, across, back], running)
    running, middle, far_back, far_ahead = lax.optimization_barrier((running, middle, far_back, far_ahead))
    far_middle = [by_core(far_ahead[:1], 1), by_core(far_back[1:], -1)]
    running = contract(2, *tiles, [middle, far_back, far_ahead], running)
    running, far_middle = lax.optimization_barrier((running, far_middle))
    return contract(LAST, *tiles, far_middle, running, chol)


def per_device(sizes, ci_vector, a_tiles, a_source, a_sign, b_tiles, b_source, b_sign):
    betas, chols = sizes["beta"], sizes["chol"]

    def core_other(value):
        return shifted(value, "beta", betas, lambda i: i ^ 1)

    chol = lax.axis_index("chol").astype(jnp.int32)
    width = ci_vector.shape[1] // chols
    quarter = lax.dynamic_slice_in_dim(ci_vector, chol * width, width, axis=1)
    place = jnp.stack([lax.axis_index("alpha"), lax.axis_index("beta"), chol]).astype(jnp.int32)
    pairs = jnp.concatenate([b_source.reshape(-1), b_sign.reshape(-1)])
    meta = jnp.concatenate([place, a_source.reshape(-1), a_sign.reshape(-1), pairs])
    plan, unit, b_held = gather_sources(meta, core_other(pairs), quarter, b_tiles, sizes)
    b_other = core_other(b_held)
    mine, other = gather_and_contract(plan, chol[None], unit, a_tiles, b_tiles, b_other, sizes)
    own, *pieces = merge(mine, core_other(other))
    for shift, piece in enumerate(pieces, 1):
        own = own + shifted(piece, "chol", chols, lambda i: (i + shift) % chols).astype(jnp.float32)
    return own.astype(jnp.bfloat16)


def solution(mesh):
    placed = (
        P("alpha", "beta"),
        P("chol", "alpha", None, None, None),
        P("alpha", None),
        P("alpha", None),
        P("chol", "beta", None, None, None),
        P("beta", None),
        P("beta", None),
    )
    sizes = dict(mesh.shape)

    def body(*args):
        return per_device(sizes, *args)

    return jax.shard_map(
        body,
        mesh=mesh,
        in_specs=placed,
        out_specs=P("alpha", ("beta", "chol")),
        check_vma=False,
    )
```

```python
import functools

import jax
import jax.numpy as jnp
from jax import lax
from jax.experimental import pallas as pl
from jax.experimental.pallas import tpu as pltpu
from jax.sharding import PartitionSpec as P

BLK = 128
VECTORS_PER_GROUP = 8
ALL_WIDTHS = ((2,), (4, 2), (4, 2), (2,))
X_SIZE = 4
A_SLOTS, B_SLOTS, B_BLOCKS = 6, 3, 8
PAIRS = B_SLOTS * B_BLOCKS
ALPHA, BETA, CHOL, A_SOURCE = 0, 1, 2, 3
A_SIGN = A_SOURCE + A_SLOTS
B_SOURCE = A_SIGN + A_SLOTS
B_SIGN = B_SOURCE + PAIRS
OTHER = 2 * PAIRS
ARRIVAL = 0x67521430
FIRST_UNITS = (0, 1, 4, 7, 8)
KERNELS = len(FIRST_UNITS) - 1
LAST = KERNELS - 1
PLAN = 64
SMEM = pl.BlockSpec(memory_space=pltpu.SMEM)
VMEM = pl.BlockSpec(memory_space=pltpu.VMEM)
HBM = pl.BlockSpec(memory_space=pltpu.HBM)


def shifted(value, axis, size, moves_to):
    return lax.ppermute(value, axis, [(i, moves_to(i)) for i in range(size)])


def choose(index, low, high, act):
    if high - low == 1:
        act(low)
        return
    middle = (low + high) // 2

    @pl.when(index < middle)
    def _():
        choose(index, low, middle, act)

    @pl.when(index >= middle)
    def _():
        choose(index, middle, high, act)


def flip_kernel(a_hbm, out_ref, a_buf, sems):
    parts = sems.shape[0]
    size = a_buf.shape[0] // parts
    copies = [
        pltpu.make_async_copy(a_hbm.at[pl.ds(p * size, size)], a_buf.at[pl.ds(p * size, size)], sems.at[p])
        for p in range(parts)
    ]
    for copy in copies:
        copy.start()
    for p, copy in enumerate(copies):
        copy.wait()
        for q in range(p * size, (p + 1) * size):
            for k in range(A_SLOTS):
                out_ref[k * BLK : (k + 1) * BLK, q * BLK : (q + 1) * BLK] = a_buf[q, 0, k].T


def plan_kernel(meta_ref, plan_ref):
    beta, chol = meta_ref[BETA], meta_ref[CHOL]
    core = beta & 1
    counts = [jnp.int32(0)] * KERNELS
    for pair in range(2 * PAIRS):
        base = OTHER if pair >= PAIRS else 0
        m = meta_ref[B_SOURCE + base + pair % PAIRS]
        sign = meta_ref[B_SIGN + base + pair % PAIRS]
        owner = m >> 3
        dy = ((m >> 1) - chol) & 3
        dy = jnp.where(core != 0, (4 - dy) & 3, dy)
        unit = (jnp.int32(ARRIVAL) >> (4 * (((owner ^ beta) & 2) * 2 + dy))) & 7
        live = (sign != 0) & ((owner & 1) == core)
        for index in range(KERNELS):
            low, high = FIRST_UNITS[index], FIRST_UNITS[index + 1]
            entry = pair + ((unit - low) << 6) + ((m & 1) << 9) + ((sign + 1) << 10)
            plan_ref[index * PLAN + 1 + counts[index]] = entry
            counts[index] = counts[index] + jnp.where(live & (unit >= low) & (unit < high), 1, 0)
    for index in range(KERNELS):
        plan_ref[index * PLAN] = counts[index]


def pick_kernel(meta_ref, own_ref, back_ref, far_ref, ahead_ref, out_ref):
    alpha = meta_ref[ALPHA]
    core = meta_ref[BETA] & 1

    def place(k, carry):
        source = meta_ref[A_SOURCE + k]
        sign = meta_ref[A_SIGN + k].astype(jnp.float32).astype(out_ref.dtype)
        dz = ((source >> 2) - (alpha >> 2)) & 3
        dx = (source - alpha) & 3
        dx = jnp.where(core != 0, (4 - dx) & 3, dx)
        lanes = pl.ds(pl.multiple_of(k * BLK, BLK), BLK)

        def put(i):
            for half in range(2):
                block = (own_ref, back_ref, far_ref, ahead_ref)[i][dz, :, half * BLK : (half + 1) * BLK]
                out_ref[half, :, lanes] = block.T * sign

        choose(dx, 0, X_SIZE, put)
        return carry

    lax.fori_loop(0, A_SLOTS, place, 0)


def contract_kernel(index, plan_ref, a_ref, b_own, b_other, *rest):
    count_units = FIRST_UNITS[index + 1] - FIRST_UNITS[index]
    units, rest = rest[:count_units], rest[count_units:]
    if index:
        sum_ref, rest = rest[0], rest[1:]
    if index == LAST:
        chol_ref, mine_ref, other_ref, acc, c_buf, b_buf, b_sem = rest
    else:
        acc, c_buf, b_buf, b_sem = rest
    widths = ALL_WIDTHS[index]
    vectors = b_own.shape[0]
    count = plan_ref[index * PLAN]
    ends, firsts, taken, steps = [], [], jnp.int32(0), jnp.int32(0)
    for width in widths:
        firsts.append(taken - width * steps)
        more = jnp.maximum(count - taken + 1, 0) // width
        taken, steps = taken + width * more, steps + more
        ends.append(steps)

    def first_of(step):
        first = firsts[-1] + widths[-1] * step
        for width, base, end in reversed(tuple(zip(widths[:-1], firsts, ends))):
            first = jnp.where(step < end, base + width * step, first)
        return first

    def entry_of(at):
        return plan_ref[index * PLAN + 1 + jnp.minimum(at, count - 1)]

    def b_copy(ref, u, l, slot, lane, part):
        vectors_of = (pl.ds(0, VECTORS_PER_GROUP), pl.ds(VECTORS_PER_GROUP, vectors - VECTORS_PER_GROUP))[part]
        return pltpu.make_async_copy(
            ref.at[vectors_of, u, l], b_buf.at[slot, lane, vectors_of], b_sem.at[slot, lane, part]
        )

    def start_b(step, slot, lanes, part):
        for lane in lanes:
            entry = entry_of(first_of(step) + lane)
            pair = entry & 63
            foreign = pair >= PAIRS
            pair = jnp.where(foreign, pair - PAIRS, pair)
            u = pair // B_SLOTS
            l = pair - u * B_SLOTS

            @pl.when(foreign)
            def _(u=u, l=l, lane=lane):
                b_copy(b_other, u, l, slot, lane, part).start()

            @pl.when(jnp.logical_not(foreign))
            def _(u=u, l=l, lane=lane):
                b_copy(b_own, u, l, slot, lane, part).start()

    def start_step(step, slot):
        def start(lanes):
            for part in range(2):
                start_b(step, slot, lanes, part)

        begin = 0
        for width, end in zip(widths, ends):

            @pl.when((step >= begin) & (step < end))
            def _(width=width):
                start(range(width))

            begin = end

    start_step(0, 0)
    acc[...] = sum_ref[...] if index else jnp.zeros_like(acc)

    def body(width, step, carry):
        slot = step & 1
        start_step(step + 1, 1 - slot)
        for lane in range(width):
            entry = entry_of(first_of(step) + lane)
            half = (entry >> 9) & 1

            def fill(i, lane=lane, half=half):
                c_buf[lane * BLK : (lane + 1) * BLK] = units[i][half]

            choose((entry >> 6) & 7, 0, count_units, fill)
        sums = [jnp.zeros((BLK, BLK), jnp.float32) for _ in range(width)]

        def panel_of(group):
            columns = slice(group * BLK, (group + VECTORS_PER_GROUP) * BLK)
            return jnp.dot(
                c_buf[: width * BLK], a_ref[:, columns], preferred_element_type=jnp.float32
            ).astype(jnp.bfloat16)

        panel = panel_of(0)
        for group in range(0, vectors, VECTORS_PER_GROUP):
            following = panel_of(group + VECTORS_PER_GROUP) if group + VECTORS_PER_GROUP < vectors else None
            if group <= VECTORS_PER_GROUP:
                for lane in range(width):
                    b_copy(b_own, 0, 0, slot, lane, group // VECTORS_PER_GROUP).wait()
            for lane in range(width):
                tiles = [b_buf[slot, lane, group + r] for r in range(VECTORS_PER_GROUP)]
                blocks = [
                    panel[lane * BLK : (lane + 1) * BLK, r * BLK : (r + 1) * BLK]
                    for r in range(VECTORS_PER_GROUP)
                ]
                sums[lane] += jnp.dot(
                    jnp.concatenate(tiles, axis=1),
                    jnp.concatenate(blocks, axis=0),
                    preferred_element_type=jnp.float32,
                )
            panel = following
        for lane in range(width):
            at = first_of(step) + lane
            entry = entry_of(at)
            factor = jnp.where(at < count, (entry >> 10) - 1, 0).astype(jnp.float32)
            acc[(entry & 63) // B_SLOTS] += factor * sums[lane]
        return carry

    begin = 0
    for width, end in zip(widths, ends):
        lax.fori_loop(begin, end, functools.partial(body, width), 0)
        begin = end
    if index == LAST:
        for shift in range(4):
            for half in range(2):
                u = ((chol_ref[0] + shift) & 3) * 2 + half
                lanes = slice(half * BLK, (half + 1) * BLK)
                mine_ref[shift, :, lanes] = acc[u].T
                other_ref[shift, :, lanes] = acc[B_BLOCKS + u].T


def contract(index, plan, a_flipped, b_own, b_other, units, running=None, chol=None):
    vectors, blocks = b_own.shape[:2]
    last = index == LAST
    widest = ALL_WIDTHS[index][0]
    part = (FIRST_UNITS[index + 1] - FIRST_UNITS[index]) / 8
    flops = int(part * 2 * (a_flipped.size * blocks * B_SLOTS * BLK + b_own.size * BLK))
    moved = int(part * 2 * b_own.size) + 2 * a_flipped.size
    whole = jax.ShapeDtypeStruct((2 * blocks, BLK, BLK), jnp.float32)
    shares = jax.ShapeDtypeStruct((4, BLK, blocks * BLK // 4), jnp.float32)
    sums = [] if running is None else [running]
    chols = [chol] if last else []
    return pl.pallas_call(
        functools.partial(contract_kernel, index),
        out_shape=[shares, shares] if last else whole,
        in_specs=[SMEM, VMEM, HBM, HBM] + [VMEM] * (len(units) + len(sums)) + [SMEM] * len(chols),
        out_specs=[VMEM, VMEM] if last else VMEM,
        scratch_shapes=[pltpu.VMEM(whole.shape, jnp.float32)] * last
        + [
            pltpu.VMEM((widest * BLK, A_SLOTS * BLK), jnp.bfloat16),
            pltpu.VMEM((2, widest, vectors, BLK, BLK), jnp.bfloat16),
            pltpu.SemaphoreType.DMA((2, widest, 2)),
        ],
        compiler_params=pltpu.CompilerParams(vmem_limit_bytes=47 * 1024 * 1024),
        cost_estimate=pl.CostEstimate(flops=flops, bytes_accessed=moved, transcendentals=0),
    )(plan, a_flipped, b_own, b_other, *units, *sums, *chols)


def merge_kernel(mine_ref, arrived_ref, own_ref, *piece_refs):
    own_ref[...] = mine_ref[0] + arrived_ref[0]
    for shift, piece_ref in enumerate(piece_refs, 1):
        piece_ref[...] = (mine_ref[shift] + arrived_ref[shift]).astype(piece_ref.dtype)


def merge(mine, arrived):
    shape = mine.shape[1:]
    return pl.pallas_call(
        merge_kernel,
        out_shape=[jax.ShapeDtypeStruct(shape, jnp.float32)] + [jax.ShapeDtypeStruct(shape, jnp.bfloat16)] * 3,
        in_specs=[VMEM, VMEM],
        out_specs=[VMEM] * 4,
        compiler_params=pltpu.CompilerParams(vmem_limit_bytes=8 * 1024 * 1024),
    )(mine, arrived)


def flip(a_tiles):
    vectors = a_tiles.shape[0]
    return pl.pallas_call(
        flip_kernel,
        out_shape=jax.ShapeDtypeStruct((A_SLOTS * BLK, vectors * BLK), a_tiles.dtype),
        in_specs=[HBM],
        out_specs=VMEM,
        scratch_shapes=[pltpu.VMEM(a_tiles.shape, a_tiles.dtype), pltpu.SemaphoreType.DMA((4,))],
        compiler_params=pltpu.CompilerParams(vmem_limit_bytes=48 * 1024 * 1024),
        cost_estimate=pl.CostEstimate(flops=0, bytes_accessed=4 * a_tiles.size, transcendentals=0),
    )(a_tiles)


def make_plan(meta):
    return pl.pallas_call(
        plan_kernel,
        out_shape=jax.ShapeDtypeStruct((KERNELS * PLAN,), jnp.int32),
        in_specs=[SMEM],
        out_specs=SMEM,
    )(meta)


def gather_sources(meta, other_pairs, quarter, b_tiles, sizes):
    alphas, betas = sizes["alpha"], sizes["beta"]
    zs = alphas // X_SIZE

    def z_from(value, distance):
        return shifted(value, "alpha", alphas, lambda i: (i // X_SIZE - distance) % zs * X_SIZE + i % X_SIZE)

    def by_core(value, sense):
        def moved(i):
            alpha, beta = i // betas, i % betas
            x = (alpha + (sense if beta % 2 == 0 else -sense)) % X_SIZE
            return (alpha // X_SIZE * X_SIZE + x) * betas + beta

        return shifted(value, ("alpha", "beta"), alphas * betas, moved)

    others = [z_from(quarter, distance) for distance in (1, 2, 3)]
    others, other_pairs, b_held = lax.optimization_barrier((others, other_pairs, b_tiles))
    meta = jnp.concatenate([meta, other_pairs])
    own = jnp.stack([quarter] + others)
    ahead, back = by_core(own, 1), by_core(own, -1)
    ahead, plan = lax.optimization_barrier((ahead, make_plan(meta)))
    far = by_core(ahead, 1)
    unit = pl.pallas_call(
        pick_kernel,
        out_shape=jax.ShapeDtypeStruct((2, BLK, A_SLOTS * BLK), quarter.dtype),
        in_specs=[SMEM] + [VMEM] * X_SIZE,
        out_specs=VMEM,
        compiler_params=pltpu.CompilerParams(vmem_limit_bytes=8 * 1024 * 1024),
    )(meta, own, back, far, ahead)
    return plan, unit, b_held


def gather_and_contract(plan, chol, unit, a_tiles, b_own, b_other, sizes):
    betas, chols = sizes["beta"], sizes["chol"]

    def z_other(value):
        return shifted(value, "beta", betas, lambda i: i ^ 2)

    def by_core(value, sense):
        def moved(i):
            beta, chol = i // chols, i % chols
            return beta * chols + (chol + (sense if beta % 2 == 0 else -sense)) % chols

        return shifted(value, ("beta", "chol"), betas * chols, moved)

    ahead, across, back = by_core(unit, 1), z_other(unit), by_core(unit, -1)
    tiles = (plan, flip(a_tiles), b_own, b_other)
    running = contract(0, *tiles, [unit])
    running, ahead, across, back = lax.optimization_barrier((running, ahead, across, back))
    middle, far_ahead, far_back = by_core(ahead, 1), z_other(ahead), by_core(across, -1)
    running = contract(1, *tiles, [ahead, across, back], running)
    running, middle, far_back, far_ahead = lax.optimization_barrier((running, middle, far_back, far_ahead))
    far_middle = by_core(far_ahead, 1)
    running = contract(2, *tiles, [middle, far_back, far_ahead], running)
    running, far_middle = lax.optimization_barrier((running, far_middle))
    return contract(LAST, *tiles, [far_middle], running, chol)


def per_device(sizes, ci_vector, a_tiles, a_source, a_sign, b_tiles, b_source, b_sign):
    betas, chols = sizes["beta"], sizes["chol"]

    def core_other(value):
        return shifted(value, "beta", betas, lambda i: i ^ 1)

    chol = lax.axis_index("chol").astype(jnp.int32)
    width = ci_vector.shape[1] // chols
    quarter = lax.dynamic_slice_in_dim(ci_vector, chol * width, width, axis=1)
    place = jnp.stack([lax.axis_index("alpha"), lax.axis_index("beta"), chol]).astype(jnp.int32)
    pairs = jnp.concatenate([b_source.reshape(-1), b_sign.reshape(-1)])
    meta = jnp.concatenate([place, a_source.reshape(-1), a_sign.reshape(-1), pairs])
    plan, unit, b_held = gather_sources(meta, core_other(pairs), quarter, b_tiles, sizes)
    b_other = core_other(b_held)
    mine, other = gather_and_contract(plan, chol[None], unit, a_tiles, b_tiles, b_other, sizes)
    own, *pieces = merge(mine, core_other(other))
    for shift, piece in enumerate(pieces, 1):
        own = own + shifted(piece, "chol", chols, lambda i: (i + shift) % chols).astype(jnp.float32)
    return own.astype(jnp.bfloat16)


def solution(mesh):
    placed = (
        P("alpha", "beta"),
        P("chol", "alpha", None, None, None),
        P("alpha", None),
        P("alpha", None),
        P("chol", "beta", None, None, None),
        P("beta", None),
        P("beta", None),
    )
    sizes = dict(mesh.shape)

    def body(*args):
        return per_device(sizes, *args)

    return jax.shard_map(
        body,
        mesh=mesh,
        in_specs=placed,
        out_specs=P("alpha", ("beta", "chol")),
        check_vma=False,
    )
```

```python
import functools

import jax
import jax.numpy as jnp
from jax import lax
from jax.experimental import pallas as pl
from jax.experimental.pallas import tpu as pltpu
from jax.sharding import PartitionSpec as P

BLK = 128
VECTORS_PER_GROUP = 8
ALL_WIDTHS = ((2,), (4, 2), (4, 2), (2,))
X_SIZE = 4
A_SLOTS, B_SLOTS, B_BLOCKS = 6, 3, 8
PAIRS = B_SLOTS * B_BLOCKS
ALPHA, BETA, CHOL, A_SOURCE = 0, 1, 2, 3
A_SIGN = A_SOURCE + A_SLOTS
B_SOURCE = A_SIGN + A_SLOTS
B_SIGN = B_SOURCE + PAIRS
OTHER = 2 * PAIRS
ARRIVAL = 0x67521430
FIRST_UNITS = (0, 1, 4, 7, 8)
KERNELS = len(FIRST_UNITS) - 1
LAST = KERNELS - 1
PLAN = 64
SMEM = pl.BlockSpec(memory_space=pltpu.SMEM)
VMEM = pl.BlockSpec(memory_space=pltpu.VMEM)
HBM = pl.BlockSpec(memory_space=pltpu.HBM)


def shifted(value, axis, size, moves_to):
    return lax.ppermute(value, axis, [(i, moves_to(i)) for i in range(size)])


def choose(index, low, high, act):
    if high - low == 1:
        act(low)
        return
    middle = (low + high) // 2

    @pl.when(index < middle)
    def _():
        choose(index, low, middle, act)

    @pl.when(index >= middle)
    def _():
        choose(index, middle, high, act)


def flip_kernel(a_hbm, out_ref, a_buf, sems):
    parts = sems.shape[0]
    size = a_buf.shape[0] // parts
    copies = [
        pltpu.make_async_copy(a_hbm.at[pl.ds(p * size, size)], a_buf.at[pl.ds(p * size, size)], sems.at[p])
        for p in range(parts)
    ]
    for copy in copies:
        copy.start()
    for p, copy in enumerate(copies):
        copy.wait()
        for q in range(p * size, (p + 1) * size):
            for k in range(A_SLOTS):
                out_ref[k * BLK : (k + 1) * BLK, q * BLK : (q + 1) * BLK] = a_buf[q, 0, k].T


def plan_kernel(meta_ref, plan_ref):
    beta, chol = meta_ref[BETA], meta_ref[CHOL]
    core = beta & 1
    counts = [jnp.int32(0)] * KERNELS
    for pair in range(2 * PAIRS):
        base = OTHER if pair >= PAIRS else 0
        m = meta_ref[B_SOURCE + base + pair % PAIRS]
        sign = meta_ref[B_SIGN + base + pair % PAIRS]
        owner = m >> 3
        dy = ((m >> 1) - chol) & 3
        dy = jnp.where(core != 0, (4 - dy) & 3, dy)
        unit = (jnp.int32(ARRIVAL) >> (4 * (((owner ^ beta) & 2) * 2 + dy))) & 7
        live = (sign != 0) & ((owner & 1) == core)
        for index in range(KERNELS):
            low, high = FIRST_UNITS[index], FIRST_UNITS[index + 1]
            where = jnp.where(unit >= 6, (unit - low + (m & 1)) << 6, ((unit - low) << 6) + ((m & 1) << 9))
            entry = pair + where + ((sign + 1) << 10)
            plan_ref[index * PLAN + 1 + counts[index]] = entry
            counts[index] = counts[index] + jnp.where(live & (unit >= low) & (unit < high), 1, 0)
    for index in range(KERNELS):
        plan_ref[index * PLAN] = counts[index]


def pick_kernel(meta_ref, own_ref, back_ref, far_ref, ahead_ref, out_ref):
    alpha = meta_ref[ALPHA]
    core = meta_ref[BETA] & 1

    def place(k, carry):
        source = meta_ref[A_SOURCE + k]
        sign = meta_ref[A_SIGN + k].astype(jnp.float32).astype(out_ref.dtype)
        dz = ((source >> 2) - (alpha >> 2)) & 3
        dx = (source - alpha) & 3
        dx = jnp.where(core != 0, (4 - dx) & 3, dx)
        lanes = pl.ds(pl.multiple_of(k * BLK, BLK), BLK)

        def put(i):
            for half in range(2):
                block = (own_ref, back_ref, far_ref, ahead_ref)[i][dz, :, half * BLK : (half + 1) * BLK]
                out_ref[half, :, lanes] = block.T * sign

        choose(dx, 0, X_SIZE, put)
        return carry

    lax.fori_loop(0, A_SLOTS, place, 0)


def contract_kernel(index, plan_ref, a_ref, b_own, b_other, *rest):
    count_units = FIRST_UNITS[index + 1] - FIRST_UNITS[index] + (index >= 2)
    units, rest = rest[:count_units], rest[count_units:]
    if index:
        sum_ref, rest = rest[0], rest[1:]
    if index == LAST:
        chol_ref, mine_ref, other_ref, acc, c_buf, b_buf, b_sem = rest
    else:
        acc, c_buf, b_buf, b_sem = rest
    widths = ALL_WIDTHS[index]
    vectors = b_own.shape[0]
    count = plan_ref[index * PLAN]
    ends, firsts, taken, steps = [], [], jnp.int32(0), jnp.int32(0)
    for width in widths:
        firsts.append(taken - width * steps)
        more = jnp.maximum(count - taken + 1, 0) // width
        taken, steps = taken + width * more, steps + more
        ends.append(steps)

    def first_of(step):
        first = firsts[-1] + widths[-1] * step
        for width, base, end in reversed(tuple(zip(widths[:-1], firsts, ends))):
            first = jnp.where(step < end, base + width * step, first)
        return first

    def entry_of(at):
        return plan_ref[index * PLAN + 1 + jnp.minimum(at, count - 1)]

    def b_copy(ref, u, l, slot, lane, part):
        vectors_of = (pl.ds(0, VECTORS_PER_GROUP), pl.ds(VECTORS_PER_GROUP, vectors - VECTORS_PER_GROUP))[part]
        return pltpu.make_async_copy(
            ref.at[vectors_of, u, l], b_buf.at[slot, lane, vectors_of], b_sem.at[slot, lane, part]
        )

    def start_b(step, slot, lanes, part):
        for lane in lanes:
            entry = entry_of(first_of(step) + lane)
            pair = entry & 63
            foreign = pair >= PAIRS
            pair = jnp.where(foreign, pair - PAIRS, pair)
            u = pair // B_SLOTS
            l = pair - u * B_SLOTS

            @pl.when(foreign)
            def _(u=u, l=l, lane=lane):
                b_copy(b_other, u, l, slot, lane, part).start()

            @pl.when(jnp.logical_not(foreign))
            def _(u=u, l=l, lane=lane):
                b_copy(b_own, u, l, slot, lane, part).start()

    def start_step(step, slot):
        def start(lanes):
            for part in range(2):
                start_b(step, slot, lanes, part)

        begin = 0
        for width, end in zip(widths, ends):

            @pl.when((step >= begin) & (step < end))
            def _(width=width):
                start(range(width))

            begin = end

    start_step(0, 0)
    acc[...] = sum_ref[...] if index else jnp.zeros_like(acc)

    def body(width, step, carry):
        slot = step & 1
        start_step(step + 1, 1 - slot)
        for lane in range(width):
            entry = entry_of(first_of(step) + lane)
            half = (entry >> 9) & 1

            def fill(i, lane=lane, half=half):
                c_buf[lane * BLK : (lane + 1) * BLK] = units[i][half]

            choose((entry >> 6) & 7, 0, count_units, fill)
        sums = [jnp.zeros((BLK, BLK), jnp.float32) for _ in range(width)]

        def panel_of(group):
            columns = slice(group * BLK, (group + VECTORS_PER_GROUP) * BLK)
            return jnp.dot(
                c_buf[: width * BLK], a_ref[:, columns], preferred_element_type=jnp.float32
            ).astype(jnp.bfloat16)

        panel = panel_of(0)
        for group in range(0, vectors, VECTORS_PER_GROUP):
            following = panel_of(group + VECTORS_PER_GROUP) if group + VECTORS_PER_GROUP < vectors else None
            if group <= VECTORS_PER_GROUP:
                for lane in range(width):
                    b_copy(b_own, 0, 0, slot, lane, group // VECTORS_PER_GROUP).wait()
            for lane in range(width):
                tiles = [b_buf[slot, lane, group + r] for r in range(VECTORS_PER_GROUP)]
                blocks = [
                    panel[lane * BLK : (lane + 1) * BLK, r * BLK : (r + 1) * BLK]
                    for r in range(VECTORS_PER_GROUP)
                ]
                sums[lane] += jnp.dot(
                    jnp.concatenate(tiles, axis=1),
                    jnp.concatenate(blocks, axis=0),
                    preferred_element_type=jnp.float32,
                )
            panel = following
        for lane in range(width):
            at = first_of(step) + lane
            entry = entry_of(at)
            factor = jnp.where(at < count, (entry >> 10) - 1, 0).astype(jnp.float32)
            acc[(entry & 63) // B_SLOTS] += factor * sums[lane]
        return carry

    begin = 0
    for width, end in zip(widths, ends):
        lax.fori_loop(begin, end, functools.partial(body, width), 0)
        begin = end
    if index == LAST:
        for shift in range(4):
            for half in range(2):
                u = ((chol_ref[0] + shift) & 3) * 2 + half
                lanes = slice(half * BLK, (half + 1) * BLK)
                mine_ref[shift, :, lanes] = acc[u].T
                other_ref[shift, :, lanes] = acc[B_BLOCKS + u].T


def contract(index, plan, a_flipped, b_own, b_other, units, running=None, chol=None):
    vectors, blocks = b_own.shape[:2]
    last = index == LAST
    widest = ALL_WIDTHS[index][0]
    part = (FIRST_UNITS[index + 1] - FIRST_UNITS[index]) / 8
    flops = int(part * 2 * (a_flipped.size * blocks * B_SLOTS * BLK + b_own.size * BLK))
    moved = int(part * 2 * b_own.size) + 2 * a_flipped.size
    whole = jax.ShapeDtypeStruct((2 * blocks, BLK, BLK), jnp.float32)
    shares = jax.ShapeDtypeStruct((4, BLK, blocks * BLK // 4), jnp.float32)
    sums = [] if running is None else [running]
    chols = [chol] if last else []
    return pl.pallas_call(
        functools.partial(contract_kernel, index),
        out_shape=[shares, shares] if last else whole,
        in_specs=[SMEM, VMEM, HBM, HBM] + [VMEM] * (len(units) + len(sums)) + [SMEM] * len(chols),
        out_specs=[VMEM, VMEM] if last else VMEM,
        scratch_shapes=[pltpu.VMEM(whole.shape, jnp.float32)] * last
        + [
            pltpu.VMEM((widest * BLK, A_SLOTS * BLK), jnp.bfloat16),
            pltpu.VMEM((2, widest, vectors, BLK, BLK), jnp.bfloat16),
            pltpu.SemaphoreType.DMA((2, widest, 2)),
        ],
        compiler_params=pltpu.CompilerParams(vmem_limit_bytes=47 * 1024 * 1024),
        cost_estimate=pl.CostEstimate(flops=flops, bytes_accessed=moved, transcendentals=0),
    )(plan, a_flipped, b_own, b_other, *units, *sums, *chols)


def merge_kernel(mine_ref, arrived_ref, own_ref, *piece_refs):
    own_ref[...] = mine_ref[0] + arrived_ref[0]
    for shift, piece_ref in enumerate(piece_refs, 1):
        piece_ref[...] = (mine_ref[shift] + arrived_ref[shift]).astype(piece_ref.dtype)


def merge(mine, arrived):
    shape = mine.shape[1:]
    return pl.pallas_call(
        merge_kernel,
        out_shape=[jax.ShapeDtypeStruct(shape, jnp.float32)] + [jax.ShapeDtypeStruct(shape, jnp.bfloat16)] * 3,
        in_specs=[VMEM, VMEM],
        out_specs=[VMEM] * 4,
        compiler_params=pltpu.CompilerParams(vmem_limit_bytes=8 * 1024 * 1024),
    )(mine, arrived)


def flip(a_tiles):
    vectors = a_tiles.shape[0]
    return pl.pallas_call(
        flip_kernel,
        out_shape=jax.ShapeDtypeStruct((A_SLOTS * BLK, vectors * BLK), a_tiles.dtype),
        in_specs=[HBM],
        out_specs=VMEM,
        scratch_shapes=[pltpu.VMEM(a_tiles.shape, a_tiles.dtype), pltpu.SemaphoreType.DMA((4,))],
        compiler_params=pltpu.CompilerParams(vmem_limit_bytes=48 * 1024 * 1024),
        cost_estimate=pl.CostEstimate(flops=0, bytes_accessed=4 * a_tiles.size, transcendentals=0),
    )(a_tiles)


def make_plan(meta):
    return pl.pallas_call(
        plan_kernel,
        out_shape=jax.ShapeDtypeStruct((KERNELS * PLAN,), jnp.int32),
        in_specs=[SMEM],
        out_specs=SMEM,
    )(meta)


def gather_sources(meta, other_pairs, quarter, b_tiles, sizes):
    alphas, betas = sizes["alpha"], sizes["beta"]
    zs = alphas // X_SIZE

    def z_from(value, distance):
        return shifted(value, "alpha", alphas, lambda i: (i // X_SIZE - distance) % zs * X_SIZE + i % X_SIZE)

    def by_core(value, sense):
        def moved(i):
            alpha, beta = i // betas, i % betas
            x = (alpha + (sense if beta % 2 == 0 else -sense)) % X_SIZE
            return (alpha // X_SIZE * X_SIZE + x) * betas + beta

        return shifted(value, ("alpha", "beta"), alphas * betas, moved)

    others = [z_from(quarter, distance) for distance in (1, 2, 3)]
    others, other_pairs, b_held = lax.optimization_barrier((others, other_pairs, b_tiles))
    meta = jnp.concatenate([meta, other_pairs])
    own = jnp.stack([quarter] + others)
    ahead, back = by_core(own, 1), by_core(own, -1)
    ahead, plan = lax.optimization_barrier((ahead, make_plan(meta)))
    far = by_core(ahead, 1)
    unit = pl.pallas_call(
        pick_kernel,
        out_shape=jax.ShapeDtypeStruct((2, BLK, A_SLOTS * BLK), quarter.dtype),
        in_specs=[SMEM] + [VMEM] * X_SIZE,
        out_specs=VMEM,
        compiler_params=pltpu.CompilerParams(vmem_limit_bytes=8 * 1024 * 1024),
    )(meta, own, back, far, ahead)
    return plan, unit, b_held


def gather_and_contract(plan, chol, unit, a_tiles, b_own, b_other, sizes):
    betas, chols = sizes["beta"], sizes["chol"]

    def z_other(value):
        return shifted(value, "beta", betas, lambda i: i ^ 2)

    def by_core(value, sense):
        def moved(i):
            beta, chol = i // chols, i % chols
            return beta * chols + (chol + (sense if beta % 2 == 0 else -sense)) % chols

        return shifted(value, ("beta", "chol"), betas * chols, moved)

    ahead, across, back = by_core(unit, 1), z_other(unit), by_core(unit, -1)
    tiles = (plan, flip(a_tiles), b_own, b_other)
    running = contract(0, *tiles, [unit])
    running, ahead, across, back = lax.optimization_barrier((running, ahead, across, back))
    middle, far_back = by_core(ahead, 1), by_core(across, -1)
    far_low, far_high = z_other(ahead[:1]), z_other(ahead[1:])
    running = contract(1, *tiles, [ahead, across, back], running)
    running, far_low = lax.optimization_barrier((running, far_low))
    last_low = by_core(far_low, 1)
    running, middle, far_back, far_high = lax.optimization_barrier((running, middle, far_back, far_high))
    last_high = by_core(far_high, 1)
    running = contract(2, *tiles, [middle, far_back, far_low, far_high], running)
    running, last_low, last_high = lax.optimization_barrier((running, last_low, last_high))
    return contract(LAST, *tiles, [last_low, last_high], running, chol)


def per_device(sizes, ci_vector, a_tiles, a_source, a_sign, b_tiles, b_source, b_sign):
    betas, chols = sizes["beta"], sizes["chol"]

    def core_other(value):
        return shifted(value, "beta", betas, lambda i: i ^ 1)

    chol = lax.axis_index("chol").astype(jnp.int32)
    width = ci_vector.shape[1] // chols
    quarter = lax.dynamic_slice_in_dim(ci_vector, chol * width, width, axis=1)
    place = jnp.stack([lax.axis_index("alpha"), lax.axis_index("beta"), chol]).astype(jnp.int32)
    pairs = jnp.concatenate([b_source.reshape(-1), b_sign.reshape(-1)])
    meta = jnp.concatenate([place, a_source.reshape(-1), a_sign.reshape(-1), pairs])
    plan, unit, b_held = gather_sources(meta, core_other(pairs), quarter, b_tiles, sizes)
    b_other = core_other(b_held)
    mine, other = gather_and_contract(plan, chol[None], unit, a_tiles, b_tiles, b_other, sizes)
    own, *pieces = merge(mine, core_other(other))
    for shift, piece in enumerate(pieces, 1):
        own = own + shifted(piece, "chol", chols, lambda i: (i + shift) % chols).astype(jnp.float32)
    return own.astype(jnp.bfloat16)


def solution(mesh):
    placed = (
        P("alpha", "beta"),
        P("chol", "alpha", None, None, None),
        P("alpha", None),
        P("alpha", None),
        P("chol", "beta", None, None, None),
        P("beta", None),
        P("beta", None),
    )
    sizes = dict(mesh.shape)

    def body(*args):
        return per_device(sizes, *args)

    return jax.shard_map(
        body,
        mesh=mesh,
        in_specs=placed,
        out_specs=P("alpha", ("beta", "chol")),
        check_vma=False,
    )
```

```python
import functools

import jax
import jax.numpy as jnp
from jax import lax
from jax.experimental import pallas as pl
from jax.experimental.pallas import tpu as pltpu
from jax.sharding import PartitionSpec as P

BLK = 128
VECTORS_PER_GROUP = 8
ALL_WIDTHS = ((2,), (4, 2), (4, 2), (2,))
X_SIZE = 4
A_SLOTS, B_SLOTS, B_BLOCKS = 6, 3, 8
PAIRS = B_SLOTS * B_BLOCKS
ALPHA, BETA, CHOL, A_SOURCE = 0, 1, 2, 3
A_SIGN = A_SOURCE + A_SLOTS
B_SOURCE = A_SIGN + A_SLOTS
B_SIGN = B_SOURCE + PAIRS
OTHER = 2 * PAIRS
ARRIVAL = 0x67521430
FIRST_UNITS = (0, 1, 4, 7, 8)
KERNELS = len(FIRST_UNITS) - 1
LAST = KERNELS - 1
PLAN = 64
SMEM = pl.BlockSpec(memory_space=pltpu.SMEM)
VMEM = pl.BlockSpec(memory_space=pltpu.VMEM)
HBM = pl.BlockSpec(memory_space=pltpu.HBM)


def shifted(value, axis, size, moves_to):
    return lax.ppermute(value, axis, [(i, moves_to(i)) for i in range(size)])


def choose(index, low, high, act):
    if high - low == 1:
        act(low)
        return
    middle = (low + high) // 2

    @pl.when(index < middle)
    def _():
        choose(index, low, middle, act)

    @pl.when(index >= middle)
    def _():
        choose(index, middle, high, act)


def flip_kernel(a_hbm, out_ref, a_buf, sems):
    parts = sems.shape[0]
    size = a_buf.shape[0] // parts
    copies = [
        pltpu.make_async_copy(a_hbm.at[pl.ds(p * size, size)], a_buf.at[pl.ds(p * size, size)], sems.at[p])
        for p in range(parts)
    ]
    for copy in copies:
        copy.start()
    for p, copy in enumerate(copies):
        copy.wait()
        for q in range(p * size, (p + 1) * size):
            for k in range(A_SLOTS):
                out_ref[k * BLK : (k + 1) * BLK, q * BLK : (q + 1) * BLK] = a_buf[q, 0, k].T


def plan_kernel(meta_ref, plan_ref):
    beta, chol = meta_ref[BETA], meta_ref[CHOL]
    core = beta & 1
    counts = [jnp.int32(0)] * KERNELS
    for pair in range(2 * PAIRS):
        base = OTHER if pair >= PAIRS else 0
        m = meta_ref[B_SOURCE + base + pair % PAIRS]
        sign = meta_ref[B_SIGN + base + pair % PAIRS]
        owner = m >> 3
        dy = ((m >> 1) - chol) & 3
        dy = jnp.where(core != 0, (4 - dy) & 3, dy)
        unit = (jnp.int32(ARRIVAL) >> (4 * (((owner ^ beta) & 2) * 2 + dy))) & 7
        live = (sign != 0) & ((owner & 1) == core)
        for index in range(KERNELS):
            low, high = FIRST_UNITS[index], FIRST_UNITS[index + 1]
            entry = pair + ((unit - low) << 6) + ((m & 1) << 9) + ((sign + 1) << 10)
            plan_ref[index * PLAN + 1 + counts[index]] = entry
            counts[index] = counts[index] + jnp.where(live & (unit >= low) & (unit < high), 1, 0)
    for index in range(KERNELS):
        plan_ref[index * PLAN] = counts[index]


def pick_kernel(meta_ref, own_ref, back_ref, far_ref, ahead_ref, out_ref):
    alpha = meta_ref[ALPHA]
    core = meta_ref[BETA] & 1

    def place(k, carry):
        source = meta_ref[A_SOURCE + k]
        sign = meta_ref[A_SIGN + k].astype(jnp.float32).astype(out_ref.dtype)
        dz = ((source >> 2) - (alpha >> 2)) & 3
        dx = (source - alpha) & 3
        dx = jnp.where(core != 0, (4 - dx) & 3, dx)
        lanes = pl.ds(pl.multiple_of(k * BLK, BLK), BLK)

        def put(i):
            for half in range(2):
                block = (own_ref, back_ref, far_ref, ahead_ref)[i][dz, :, half * BLK : (half + 1) * BLK]
                out_ref[half, :, lanes] = block.T * sign

        choose(dx, 0, X_SIZE, put)
        return carry

    lax.fori_loop(0, A_SLOTS, place, 0)


def contract_kernel(index, plan_ref, a_ref, b_own, b_other, *rest):
    count_units = FIRST_UNITS[index + 1] - FIRST_UNITS[index]
    units, rest = rest[:count_units], rest[count_units:]
    if index:
        sum_ref, rest = rest[0], rest[1:]
    if index == LAST:
        chol_ref, mine_ref, other_ref, acc, c_buf, b_buf, b_sem = rest
    else:
        acc, c_buf, b_buf, b_sem = rest
    widths = ALL_WIDTHS[index]
    vectors = b_own.shape[0]
    count = plan_ref[index * PLAN]
    ends, firsts, taken, steps = [], [], jnp.int32(0), jnp.int32(0)
    for width in widths:
        firsts.append(taken - width * steps)
        more = jnp.maximum(count - taken + 1, 0) // width
        taken, steps = taken + width * more, steps + more
        ends.append(steps)

    def first_of(step):
        first = firsts[-1] + widths[-1] * step
        for width, base, end in reversed(tuple(zip(widths[:-1], firsts, ends))):
            first = jnp.where(step < end, base + width * step, first)
        return first

    def entry_of(at):
        return plan_ref[index * PLAN + 1 + jnp.minimum(at, count - 1)]

    def b_copy(ref, u, l, slot, lane, part):
        vectors_of = (pl.ds(0, VECTORS_PER_GROUP), pl.ds(VECTORS_PER_GROUP, vectors - VECTORS_PER_GROUP))[part]
        return pltpu.make_async_copy(
            ref.at[vectors_of, u, l], b_buf.at[slot, lane, vectors_of], b_sem.at[slot, lane, part]
        )

    def start_b(step, slot, lanes, part):
        for lane in lanes:
            entry = entry_of(first_of(step) + lane)
            pair = entry & 63
            foreign = pair >= PAIRS
            pair = jnp.where(foreign, pair - PAIRS, pair)
            u = pair // B_SLOTS
            l = pair - u * B_SLOTS

            @pl.when(foreign)
            def _(u=u, l=l, lane=lane):
                b_copy(b_other, u, l, slot, lane, part).start()

            @pl.when(jnp.logical_not(foreign))
            def _(u=u, l=l, lane=lane):
                b_copy(b_own, u, l, slot, lane, part).start()

    def start_step(step, slot):
        def start(lanes):
            for part in range(2):
                start_b(step, slot, lanes, part)

        begin = 0
        for width, end in zip(widths, ends):

            @pl.when((step >= begin) & (step < end))
            def _(width=width):
                start(range(width))

            begin = end

    start_step(0, 0)
    acc[...] = sum_ref[...] if index else jnp.zeros_like(acc)

    def body(width, step, carry):
        slot = step & 1
        start_step(step + 1, 1 - slot)
        for lane in range(width):
            entry = entry_of(first_of(step) + lane)
            half = (entry >> 9) & 1

            def fill(i, lane=lane, half=half):
                c_buf[lane * BLK : (lane + 1) * BLK] = units[i][half]

            choose((entry >> 6) & 7, 0, count_units, fill)
        sums = [jnp.zeros((BLK, BLK), jnp.float32) for _ in range(width)]

        def panel_of(group):
            columns = slice(group * BLK, (group + VECTORS_PER_GROUP) * BLK)
            return jnp.dot(
                c_buf[: width * BLK], a_ref[:, columns], preferred_element_type=jnp.float32
            ).astype(jnp.bfloat16)

        panel = panel_of(0)
        for group in range(0, vectors, VECTORS_PER_GROUP):
            following = panel_of(group + VECTORS_PER_GROUP) if group + VECTORS_PER_GROUP < vectors else None
            if group <= VECTORS_PER_GROUP:
                for lane in range(width):
                    b_copy(b_own, 0, 0, slot, lane, group // VECTORS_PER_GROUP).wait()
            for lane in range(width):
                tiles = [b_buf[slot, lane, group + r] for r in range(VECTORS_PER_GROUP)]
                blocks = [
                    panel[lane * BLK : (lane + 1) * BLK, r * BLK : (r + 1) * BLK]
                    for r in range(VECTORS_PER_GROUP)
                ]
                sums[lane] += jnp.dot(
                    jnp.concatenate(tiles, axis=1),
                    jnp.concatenate(blocks, axis=0),
                    preferred_element_type=jnp.float32,
                )
            panel = following
        for lane in range(width):
            at = first_of(step) + lane
            entry = entry_of(at)
            factor = jnp.where(at < count, (entry >> 10) - 1, 0).astype(jnp.float32)
            acc[(entry & 63) // B_SLOTS] += factor * sums[lane]
        return carry

    begin = 0
    for width, end in zip(widths, ends):
        lax.fori_loop(begin, end, functools.partial(body, width), 0)
        begin = end
    if index == LAST:
        for shift in range(4):
            for half in range(2):
                u = ((chol_ref[0] + shift) & 3) * 2 + half
                lanes = slice(half * BLK, (half + 1) * BLK)
                mine_ref[shift, :, lanes] = acc[u].T
                other_ref[shift, :, lanes] = acc[B_BLOCKS + u].T


def contract(index, plan, a_flipped, b_own, b_other, units, running=None, chol=None):
    vectors, blocks = b_own.shape[:2]
    last = index == LAST
    widest = ALL_WIDTHS[index][0]
    part = (FIRST_UNITS[index + 1] - FIRST_UNITS[index]) / 8
    flops = int(part * 2 * (a_flipped.size * blocks * B_SLOTS * BLK + b_own.size * BLK))
    moved = int(part * 2 * b_own.size) + 2 * a_flipped.size
    whole = jax.ShapeDtypeStruct((2 * blocks, BLK, BLK), jnp.float32)
    shares = jax.ShapeDtypeStruct((4, BLK, blocks * BLK // 4), jnp.float32)
    sums = [] if running is None else [running]
    chols = [chol] if last else []
    return pl.pallas_call(
        functools.partial(contract_kernel, index),
        out_shape=[shares, shares] if last else whole,
        in_specs=[SMEM, VMEM, HBM, HBM] + [VMEM] * (len(units) + len(sums)) + [SMEM] * len(chols),
        out_specs=[VMEM, VMEM] if last else VMEM,
        scratch_shapes=[pltpu.VMEM(whole.shape, jnp.float32)] * last
        + [
            pltpu.VMEM((widest * BLK, A_SLOTS * BLK), jnp.bfloat16),
            pltpu.VMEM((2, widest, vectors, BLK, BLK), jnp.bfloat16),
            pltpu.SemaphoreType.DMA((2, widest, 2)),
        ],
        compiler_params=pltpu.CompilerParams(vmem_limit_bytes=47 * 1024 * 1024),
        cost_estimate=pl.CostEstimate(flops=flops, bytes_accessed=moved, transcendentals=0),
    )(plan, a_flipped, b_own, b_other, *units, *sums, *chols)


def merge_kernel(mine_ref, arrived_ref, own_ref, *piece_refs):
    own_ref[...] = mine_ref[0] + arrived_ref[0]
    for shift, piece_ref in enumerate(piece_refs, 1):
        piece_ref[...] = (mine_ref[shift] + arrived_ref[shift]).astype(piece_ref.dtype)


def merge(mine, arrived):
    shape = mine.shape[1:]
    return pl.pallas_call(
        merge_kernel,
        out_shape=[jax.ShapeDtypeStruct(shape, jnp.float32)] + [jax.ShapeDtypeStruct(shape, jnp.bfloat16)] * 3,
        in_specs=[VMEM, VMEM],
        out_specs=[VMEM] * 4,
        compiler_params=pltpu.CompilerParams(vmem_limit_bytes=8 * 1024 * 1024),
    )(mine, arrived)


def flip(a_tiles):
    vectors = a_tiles.shape[0]
    return pl.pallas_call(
        flip_kernel,
        out_shape=jax.ShapeDtypeStruct((A_SLOTS * BLK, vectors * BLK), a_tiles.dtype),
        in_specs=[HBM],
        out_specs=VMEM,
        scratch_shapes=[pltpu.VMEM(a_tiles.shape, a_tiles.dtype), pltpu.SemaphoreType.DMA((4,))],
        compiler_params=pltpu.CompilerParams(vmem_limit_bytes=48 * 1024 * 1024),
        cost_estimate=pl.CostEstimate(flops=0, bytes_accessed=4 * a_tiles.size, transcendentals=0),
    )(a_tiles)


def make_plan(meta):
    return pl.pallas_call(
        plan_kernel,
        out_shape=jax.ShapeDtypeStruct((KERNELS * PLAN,), jnp.int32),
        in_specs=[SMEM],
        out_specs=SMEM,
    )(meta)


def gather_sources(meta, other_pairs, quarter, b_tiles, sizes):
    alphas, betas = sizes["alpha"], sizes["beta"]
    zs = alphas // X_SIZE

    def z_from(value, distance):
        return shifted(value, "alpha", alphas, lambda i: (i // X_SIZE - distance) % zs * X_SIZE + i % X_SIZE)

    def by_core(value, sense):
        def moved(i):
            alpha, beta = i // betas, i % betas
            x = (alpha + (sense if beta % 2 == 0 else -sense)) % X_SIZE
            return (alpha // X_SIZE * X_SIZE + x) * betas + beta

        return shifted(value, ("alpha", "beta"), alphas * betas, moved)

    others = [z_from(quarter, distance) for distance in (1, 2, 3)]
    others, other_pairs, b_held = lax.optimization_barrier((others, other_pairs, b_tiles))
    meta = jnp.concatenate([meta, other_pairs])
    own = jnp.stack([quarter] + others)
    ahead, back = by_core(own, 1), by_core(own, -1)
    ahead, plan = lax.optimization_barrier((ahead, make_plan(meta)))
    far = by_core(ahead, 1)
    unit = pl.pallas_call(
        pick_kernel,
        out_shape=jax.ShapeDtypeStruct((2, BLK, A_SLOTS * BLK), quarter.dtype),
        in_specs=[SMEM] + [VMEM] * X_SIZE,
        out_specs=VMEM,
        compiler_params=pltpu.CompilerParams(vmem_limit_bytes=8 * 1024 * 1024),
    )(meta, own, back, far, ahead)
    return plan, unit, b_held


def gather_and_contract(plan, chol, unit, a_tiles, b_own, b_other, sizes):
    betas, chols = sizes["beta"], sizes["chol"]

    def z_other(value):
        return shifted(value, "beta", betas, lambda i: i ^ 2)

    def by_core(value, sense):
        def moved(i):
            beta, chol = i // chols, i % chols
            return beta * chols + (chol + (sense if beta % 2 == 0 else -sense)) % chols

        return shifted(value, ("beta", "chol"), betas * chols, moved)

    ahead, across, back = by_core(unit, 1), z_other(unit), by_core(unit, -1)
    tiles = (plan, flip(a_tiles), b_own, b_other)
    running = contract(0, *tiles, [unit])
    running, ahead, across, back = lax.optimization_barrier((running, ahead, across, back))
    middle, far_ahead, far_back = by_core(ahead, 1), z_other(ahead), by_core(across, -1)
    running = contract(1, *tiles, [ahead, across, back], running)
    running, middle, far_back, far_ahead = lax.optimization_barrier((running, middle, far_back, far_ahead))
    far_middle = by_core(far_ahead, 1)
    running = contract(2, *tiles, [middle, far_back, far_ahead], running)
    running, far_middle = lax.optimization_barrier((running, far_middle))
    return contract(LAST, *tiles, [far_middle], running, chol)


def per_device(sizes, ci_vector, a_tiles, a_source, a_sign, b_tiles, b_source, b_sign):
    betas, chols = sizes["beta"], sizes["chol"]

    def core_other(value):
        return shifted(value, "beta", betas, lambda i: i ^ 1)

    chol = lax.axis_index("chol").astype(jnp.int32)
    width = ci_vector.shape[1] // chols
    quarter = lax.dynamic_slice_in_dim(ci_vector, chol * width, width, axis=1)
    place = jnp.stack([lax.axis_index("alpha"), lax.axis_index("beta"), chol]).astype(jnp.int32)
    pairs = jnp.concatenate([b_source.reshape(-1), b_sign.reshape(-1)])
    meta = jnp.concatenate([place, a_source.reshape(-1), a_sign.reshape(-1), pairs])
    plan, unit, b_held = gather_sources(meta, core_other(pairs), quarter, b_tiles, sizes)
    b_other = core_other(b_held)
    mine, other = gather_and_contract(plan, chol[None], unit, a_tiles, b_tiles, b_other, sizes)
    own, *pieces = merge(mine, core_other(other))
    for shift in (2, 1, 3):
        moved = shifted(pieces[shift - 1], "chol", chols, lambda i: (i + shift) % chols)
        own = own + moved.astype(jnp.float32)
    return own.astype(jnp.bfloat16)


def solution(mesh):
    placed = (
        P("alpha", "beta"),
        P("chol", "alpha", None, None, None),
        P("alpha", None),
        P("alpha", None),
        P("chol", "beta", None, None, None),
        P("beta", None),
        P("beta", None),
    )
    sizes = dict(mesh.shape)

    def body(*args):
        return per_device(sizes, *args)

    return jax.shard_map(
        body,
        mesh=mesh,
        in_specs=placed,
        out_specs=P("alpha", ("beta", "chol")),
        check_vma=False,
    )
```

```python
import functools

import jax
import jax.numpy as jnp
from jax import lax
from jax.experimental import pallas as pl
from jax.experimental.pallas import tpu as pltpu
from jax.sharding import PartitionSpec as P

BLK = 128
VECTORS_PER_GROUP = 8
ALL_WIDTHS = ((2,), (4, 2), (4, 2), (2,))
X_SIZE = 4
A_SLOTS, B_SLOTS, B_BLOCKS = 6, 3, 8
PAIRS = B_SLOTS * B_BLOCKS
ALPHA, BETA, CHOL, A_SOURCE = 0, 1, 2, 3
A_SIGN = A_SOURCE + A_SLOTS
B_SOURCE = A_SIGN + A_SLOTS
B_SIGN = B_SOURCE + PAIRS
OTHER = 2 * PAIRS
ARRIVAL = 0x67521430
FIRST_UNITS = (0, 1, 4, 7, 8)
KERNELS = len(FIRST_UNITS) - 1
LAST = KERNELS - 1
PLAN = 64
SMEM = pl.BlockSpec(memory_space=pltpu.SMEM)
VMEM = pl.BlockSpec(memory_space=pltpu.VMEM)
HBM = pl.BlockSpec(memory_space=pltpu.HBM)


def shifted(value, axis, size, moves_to):
    return lax.ppermute(value, axis, [(i, moves_to(i)) for i in range(size)])


def choose(index, low, high, act):
    if high - low == 1:
        act(low)
        return
    middle = (low + high) // 2

    @pl.when(index < middle)
    def _():
        choose(index, low, middle, act)

    @pl.when(index >= middle)
    def _():
        choose(index, middle, high, act)


def flip_kernel(a_hbm, out_ref, a_buf, sems):
    parts = sems.shape[0]
    size = a_buf.shape[0] // parts
    copies = [
        pltpu.make_async_copy(a_hbm.at[pl.ds(p * size, size)], a_buf.at[pl.ds(p * size, size)], sems.at[p])
        for p in range(parts)
    ]
    for copy in copies:
        copy.start()
    for p, copy in enumerate(copies):
        copy.wait()
        for q in range(p * size, (p + 1) * size):
            for k in range(A_SLOTS):
                out_ref[k * BLK : (k + 1) * BLK, q * BLK : (q + 1) * BLK] = a_buf[q, 0, k].T


def plan_kernel(meta_ref, plan_ref):
    beta, chol = meta_ref[BETA], meta_ref[CHOL]
    core = beta & 1
    counts = [jnp.int32(0)] * KERNELS
    for pair in range(2 * PAIRS):
        base = OTHER if pair >= PAIRS else 0
        m = meta_ref[B_SOURCE + base + pair % PAIRS]
        sign = meta_ref[B_SIGN + base + pair % PAIRS]
        owner = m >> 3
        dy = ((m >> 1) - chol) & 3
        dy = jnp.where(core != 0, (4 - dy) & 3, dy)
        unit = (jnp.int32(ARRIVAL) >> (4 * (((owner ^ beta) & 2) * 2 + dy))) & 7
        live = (sign != 0) & ((owner & 1) == core)
        for index in range(KERNELS):
            low, high = FIRST_UNITS[index], FIRST_UNITS[index + 1]
            entry = pair + ((unit - low) << 6) + ((m & 1) << 9) + ((sign + 1) << 10)
            plan_ref[index * PLAN + 1 + counts[index]] = entry
            counts[index] = counts[index] + jnp.where(live & (unit >= low) & (unit < high), 1, 0)
    for index in range(KERNELS):
        plan_ref[index * PLAN] = counts[index]


def pick_kernel(meta_ref, own_ref, back_ref, far_ref, ahead_ref, out_ref):
    alpha = meta_ref[ALPHA]
    core = meta_ref[BETA] & 1

    def place(k, carry):
        source = meta_ref[A_SOURCE + k]
        sign = meta_ref[A_SIGN + k].astype(jnp.float32).astype(out_ref.dtype)
        dz = ((source >> 2) - (alpha >> 2)) & 3
        dx = (source - alpha) & 3
        dx = jnp.where(core != 0, (4 - dx) & 3, dx)
        lanes = pl.ds(pl.multiple_of(k * BLK, BLK), BLK)

        def put(i):
            for half in range(2):
                block = (own_ref, back_ref, far_ref, ahead_ref)[i][dz, :, half * BLK : (half + 1) * BLK]
                out_ref[half, :, lanes] = block.T * sign

        choose(dx, 0, X_SIZE, put)
        return carry

    lax.fori_loop(0, A_SLOTS, place, 0)


def contract_kernel(index, plan_ref, a_ref, b_own, b_other, *rest):
    count_units = FIRST_UNITS[index + 1] - FIRST_UNITS[index]
    units, rest = rest[:count_units], rest[count_units:]
    if index:
        sum_ref, rest = rest[0], rest[1:]
    if index == LAST:
        chol_ref, mine_ref, other_ref, acc, c_buf, b_buf, b_sem = rest
    else:
        acc, c_buf, b_buf, b_sem = rest
    widths = ALL_WIDTHS[index]
    vectors = b_own.shape[0]
    count = plan_ref[index * PLAN]
    ends, firsts, taken, steps = [], [], jnp.int32(0), jnp.int32(0)
    for width in widths:
        firsts.append(taken - width * steps)
        more = jnp.maximum(count - taken + 1, 0) // width
        taken, steps = taken + width * more, steps + more
        ends.append(steps)

    def first_of(step):
        first = firsts[-1] + widths[-1] * step
        for width, base, end in reversed(tuple(zip(widths[:-1], firsts, ends))):
            first = jnp.where(step < end, base + width * step, first)
        return first

    def entry_of(at):
        return plan_ref[index * PLAN + 1 + jnp.minimum(at, count - 1)]

    def b_copy(ref, u, l, slot, lane, part):
        vectors_of = (pl.ds(0, VECTORS_PER_GROUP), pl.ds(VECTORS_PER_GROUP, vectors - VECTORS_PER_GROUP))[part]
        return pltpu.make_async_copy(
            ref.at[vectors_of, u, l], b_buf.at[slot, lane, vectors_of], b_sem.at[slot, lane, part]
        )

    def start_b(step, slot, lanes, part):
        for lane in lanes:
            entry = entry_of(first_of(step) + lane)
            pair = entry & 63
            foreign = pair >= PAIRS
            pair = jnp.where(foreign, pair - PAIRS, pair)
            u = pair // B_SLOTS
            l = pair - u * B_SLOTS

            @pl.when(foreign)
            def _(u=u, l=l, lane=lane):
                b_copy(b_other, u, l, slot, lane, part).start()

            @pl.when(jnp.logical_not(foreign))
            def _(u=u, l=l, lane=lane):
                b_copy(b_own, u, l, slot, lane, part).start()

    def start_step(step, slot):
        def start(lanes):
            for part in range(2):
                start_b(step, slot, lanes, part)

        begin = 0
        for width, end in zip(widths, ends):

            @pl.when((step >= begin) & (step < end))
            def _(width=width):
                start(range(width))

            begin = end

    start_step(0, 0)
    acc[...] = sum_ref[...] if index else jnp.zeros_like(acc)

    def body(width, step, carry):
        slot = step & 1
        start_step(step + 1, 1 - slot)
        for lane in range(width):
            entry = entry_of(first_of(step) + lane)
            half = (entry >> 9) & 1

            def fill(i, lane=lane, half=half):
                c_buf[lane * BLK : (lane + 1) * BLK] = units[i][half]

            choose((entry >> 6) & 7, 0, count_units, fill)
        sums = [jnp.zeros((BLK, BLK), jnp.float32) for _ in range(width)]

        def panel_of(group):
            columns = slice(group * BLK, (group + VECTORS_PER_GROUP) * BLK)
            return jnp.dot(
                c_buf[: width * BLK], a_ref[:, columns], preferred_element_type=jnp.float32
            ).astype(jnp.bfloat16)

        panel = panel_of(0)
        for group in range(0, vectors, VECTORS_PER_GROUP):
            following = panel_of(group + VECTORS_PER_GROUP) if group + VECTORS_PER_GROUP < vectors else None
            if group <= VECTORS_PER_GROUP:
                for lane in range(width):
                    b_copy(b_own, 0, 0, slot, lane, group // VECTORS_PER_GROUP).wait()
            for lane in range(width):
                tiles = [b_buf[slot, lane, group + r] for r in range(VECTORS_PER_GROUP)]
                blocks = [
                    panel[lane * BLK : (lane + 1) * BLK, r * BLK : (r + 1) * BLK]
                    for r in range(VECTORS_PER_GROUP)
                ]
                sums[lane] += jnp.dot(
                    jnp.concatenate(tiles, axis=1),
                    jnp.concatenate(blocks, axis=0),
                    preferred_element_type=jnp.float32,
                )
            panel = following
        for lane in range(width):
            at = first_of(step) + lane
            entry = entry_of(at)
            factor = jnp.where(at < count, (entry >> 10) - 1, 0).astype(jnp.float32)
            acc[(entry & 63) // B_SLOTS] += factor * sums[lane]
        return carry

    begin = 0
    for width, end in zip(widths, ends):
        lax.fori_loop(begin, end, functools.partial(body, width), 0)
        begin = end
    if index == LAST:
        for shift in range(4):
            for half in range(2):
                u = ((chol_ref[0] + shift) & 3) * 2 + half
                lanes = slice(half * BLK, (half + 1) * BLK)
                mine_ref[shift, :, lanes] = acc[u].T
                other_ref[shift, :, lanes] = acc[B_BLOCKS + u].T


def contract(index, plan, a_flipped, b_own, b_other, units, running=None, chol=None):
    vectors, blocks = b_own.shape[:2]
    last = index == LAST
    widest = ALL_WIDTHS[index][0]
    part = (FIRST_UNITS[index + 1] - FIRST_UNITS[index]) / 8
    flops = int(part * 2 * (a_flipped.size * blocks * B_SLOTS * BLK + b_own.size * BLK))
    moved = int(part * 2 * b_own.size) + 2 * a_flipped.size
    whole = jax.ShapeDtypeStruct((2 * blocks, BLK, BLK), jnp.float32)
    shares = jax.ShapeDtypeStruct((4, BLK, blocks * BLK // 4), jnp.float32)
    sums = [] if running is None else [running]
    chols = [chol] if last else []
    return pl.pallas_call(
        functools.partial(contract_kernel, index),
        out_shape=[shares, shares] if last else whole,
        in_specs=[SMEM, VMEM, HBM, HBM] + [VMEM] * (len(units) + len(sums)) + [SMEM] * len(chols),
        out_specs=[VMEM, VMEM] if last else VMEM,
        scratch_shapes=[pltpu.VMEM(whole.shape, jnp.float32)] * last
        + [
            pltpu.VMEM((widest * BLK, A_SLOTS * BLK), jnp.bfloat16),
            pltpu.VMEM((2, widest, vectors, BLK, BLK), jnp.bfloat16),
            pltpu.SemaphoreType.DMA((2, widest, 2)),
        ],
        compiler_params=pltpu.CompilerParams(vmem_limit_bytes=47 * 1024 * 1024),
        cost_estimate=pl.CostEstimate(flops=flops // (1000 if index == 2 else 1), bytes_accessed=moved // (1000 if index == 2 else 1), transcendentals=0),
    )(plan, a_flipped, b_own, b_other, *units, *sums, *chols)


def merge_kernel(mine_ref, arrived_ref, own_ref, *piece_refs):
    own_ref[...] = mine_ref[0] + arrived_ref[0]
    for shift, piece_ref in enumerate(piece_refs, 1):
        piece_ref[...] = (mine_ref[shift] + arrived_ref[shift]).astype(piece_ref.dtype)


def merge(mine, arrived):
    shape = mine.shape[1:]
    return pl.pallas_call(
        merge_kernel,
        out_shape=[jax.ShapeDtypeStruct(shape, jnp.float32)] + [jax.ShapeDtypeStruct(shape, jnp.bfloat16)] * 3,
        in_specs=[VMEM, VMEM],
        out_specs=[VMEM] * 4,
        compiler_params=pltpu.CompilerParams(vmem_limit_bytes=8 * 1024 * 1024),
    )(mine, arrived)


def flip(a_tiles):
    vectors = a_tiles.shape[0]
    return pl.pallas_call(
        flip_kernel,
        out_shape=jax.ShapeDtypeStruct((A_SLOTS * BLK, vectors * BLK), a_tiles.dtype),
        in_specs=[HBM],
        out_specs=VMEM,
        scratch_shapes=[pltpu.VMEM(a_tiles.shape, a_tiles.dtype), pltpu.SemaphoreType.DMA((4,))],
        compiler_params=pltpu.CompilerParams(vmem_limit_bytes=48 * 1024 * 1024),
        cost_estimate=pl.CostEstimate(flops=0, bytes_accessed=4 * a_tiles.size, transcendentals=0),
    )(a_tiles)


def make_plan(meta):
    return pl.pallas_call(
        plan_kernel,
        out_shape=jax.ShapeDtypeStruct((KERNELS * PLAN,), jnp.int32),
        in_specs=[SMEM],
        out_specs=SMEM,
    )(meta)


def gather_sources(meta, other_pairs, quarter, b_tiles, sizes):
    alphas, betas = sizes["alpha"], sizes["beta"]
    zs = alphas // X_SIZE

    def z_from(value, distance):
        return shifted(value, "alpha", alphas, lambda i: (i // X_SIZE - distance) % zs * X_SIZE + i % X_SIZE)

    def by_core(value, sense):
        def moved(i):
            alpha, beta = i // betas, i % betas
            x = (alpha + (sense if beta % 2 == 0 else -sense)) % X_SIZE
            return (alpha // X_SIZE * X_SIZE + x) * betas + beta

        return shifted(value, ("alpha", "beta"), alphas * betas, moved)

    others = [z_from(quarter, distance) for distance in (1, 2, 3)]
    others, other_pairs, b_held = lax.optimization_barrier((others, other_pairs, b_tiles))
    meta = jnp.concatenate([meta, other_pairs])
    own = jnp.stack([quarter] + others)
    ahead, back = by_core(own, 1), by_core(own, -1)
    ahead, plan = lax.optimization_barrier((ahead, make_plan(meta)))
    far = by_core(ahead, 1)
    unit = pl.pallas_call(
        pick_kernel,
        out_shape=jax.ShapeDtypeStruct((2, BLK, A_SLOTS * BLK), quarter.dtype),
        in_specs=[SMEM] + [VMEM] * X_SIZE,
        out_specs=VMEM,
        compiler_params=pltpu.CompilerParams(vmem_limit_bytes=8 * 1024 * 1024),
    )(meta, own, back, far, ahead)
    return plan, unit, b_held


def gather_and_contract(plan, chol, unit, a_tiles, b_own, b_other, sizes):
    betas, chols = sizes["beta"], sizes["chol"]

    def z_other(value):
        return shifted(value, "beta", betas, lambda i: i ^ 2)

    def by_core(value, sense):
        def moved(i):
            beta, chol = i // chols, i % chols
            return beta * chols + (chol + (sense if beta % 2 == 0 else -sense)) % chols

        return shifted(value, ("beta", "chol"), betas * chols, moved)

    ahead, across, back = by_core(unit, 1), z_other(unit), by_core(unit, -1)
    tiles = (plan, flip(a_tiles), b_own, b_other)
    running = contract(0, *tiles, [unit])
    running, ahead, across, back = lax.optimization_barrier((running, ahead, across, back))
    middle, far_ahead, far_back = by_core(ahead, 1), z_other(ahead), by_core(across, -1)
    running = contract(1, *tiles, [ahead, across, back], running)
    running, far_ahead = lax.optimization_barrier((running, far_ahead))
    far_middle = by_core(far_ahead, 1)
    running, middle, far_back = lax.optimization_barrier((running, middle, far_back))
    running = contract(2, *tiles, [middle, far_back, far_ahead], running)
    running, far_middle = lax.optimization_barrier((running, far_middle))
    return contract(LAST, *tiles, [far_middle], running, chol)


def per_device(sizes, ci_vector, a_tiles, a_source, a_sign, b_tiles, b_source, b_sign):
    betas, chols = sizes["beta"], sizes["chol"]

    def core_other(value):
        return shifted(value, "beta", betas, lambda i: i ^ 1)

    chol = lax.axis_index("chol").astype(jnp.int32)
    width = ci_vector.shape[1] // chols
    quarter = lax.dynamic_slice_in_dim(ci_vector, chol * width, width, axis=1)
    place = jnp.stack([lax.axis_index("alpha"), lax.axis_index("beta"), chol]).astype(jnp.int32)
    pairs = jnp.concatenate([b_source.reshape(-1), b_sign.reshape(-1)])
    meta = jnp.concatenate([place, a_source.reshape(-1), a_sign.reshape(-1), pairs])
    plan, unit, b_held = gather_sources(meta, core_other(pairs), quarter, b_tiles, sizes)
    b_other = core_other(b_held)
    mine, other = gather_and_contract(plan, chol[None], unit, a_tiles, b_tiles, b_other, sizes)
    own, *pieces = merge(mine, core_other(other))
    for shift, piece in enumerate(pieces, 1):
        own = own + shifted(piece, "chol", chols, lambda i: (i + shift) % chols).astype(jnp.float32)
    return own.astype(jnp.bfloat16)


def solution(mesh):
    placed = (
        P("alpha", "beta"),
        P("chol", "alpha", None, None, None),
        P("alpha", None),
        P("alpha", None),
        P("chol", "beta", None, None, None),
        P("beta", None),
        P("beta", None),
    )
    sizes = dict(mesh.shape)

    def body(*args):
        return per_device(sizes, *args)

    return jax.shard_map(
        body,
        mesh=mesh,
        in_specs=placed,
        out_specs=P("alpha", ("beta", "chol")),
        check_vma=False,
    )
```
